32 devices in a mesh: row: 8 (over y, x, core), col: 4 (over z).
Axes of the slice: x: 2, y: 2, z: 4, core: 2. Of those that a mesh axis runs over, the one named last changes fastest.
Arguments:
- src_latent: bfloat16 [32, 32768], P(None, 'row'), may hold values from -6 to 6
- tgt_latent: bfloat16 [32, 8192], P(None, 'col'), may hold values from -6 to 6
- g_start: float32 [8192], P('col'), may hold values from -1.5 to 1.5
- pairs: int32 [8, 4, 8, 2], P('row', 'col'), may hold values from 0 to 7, as said below
- counts: int32 [8, 4], P('row', 'col'), may hold values from 1 to 8, as said below
Outputs:
- f_new: float32 [32768], P('row')
- g_new: float32 [8192], P('col')
- bary: float32 [32, 32768], P(None, 'row')
The draws below stay inside these ranges and needn't reach their ends.
Inputs may be any that keep to these rules, and one draw needn't show every extreme that they name: Within one device's 8 slots all pairs are distinct; entry 0 is below 8 and entry 1 below 4. Every source block and every target block appears among the live slots of some device. `counts`: some device has exactly 8 live slots in every draw.
All inputs are finite; a program needn't handle non-finite values.
Results may differ from the reference program's by a relative error of at most 0.0012.
Values sent between devices are 32-bit elements; how exact they have to be, the bound alone decides.
A program may use at most 64 MiB of HBM per device.

```python
import jax
import jax.numpy as jnp
from jax import lax

DIM = 32
BLOCK = 512
SB = 8
TB = 4
PAIRS = 8
NS = 32768
NT = 8192
N_ROW = 8
N_COL = 4


def draw_counts(key, part):
    key = jax.random.fold_in(key, 11)
    devices_all = N_ROW * N_COL
    raw = jax.random.randint(key, (devices_all,), 0, PAIRS)
    cover = (SB + N_COL - 1) // N_COL
    loads = jnp.maximum(1 + raw * raw // PAIRS, cover)
    busiest = jax.random.randint(jax.random.fold_in(key, 7), (), 0, devices_all)
    loads = jnp.where(jnp.arange(devices_all) == busiest, PAIRS, loads)
    return loads.reshape(N_ROW, N_COL).astype(jnp.int32)


def draw_pairs(key, part):
    key = jax.random.fold_in(key, 13)
    cells = SB * TB
    cover = (SB + N_COL - 1) // N_COL
    rr = jnp.arange(N_ROW, dtype=jnp.int32)[:, None, None]
    cc = jnp.arange(N_COL, dtype=jnp.int32)[None, :, None]
    kk = jnp.arange(cover, dtype=jnp.int32)[None, None, :]
    forced_id = (cc + N_COL * kk) % SB * TB + (rr + kk) % TB
    ids = jnp.arange(cells, dtype=jnp.int32)
    forced = jnp.any(ids[None, None, None, :] == forced_id[..., None], axis=2)
    scores = jax.random.randint(key, (N_ROW, N_COL, cells), 0, 2 ** 20) * cells + ids[None, None, :]
    sort_key = jnp.where(forced, ids[None, None, :], cells + scores)
    order = jnp.argsort(sort_key, axis=-1)[..., :PAIRS].astype(jnp.int32)
    return jnp.stack([order // TB, order % TB], axis=-1).astype(jnp.int32)


def shard_levels(rng, dims, cuts, least, top_value):
    def one(position, shards_of):
        steps = jax.random.uniform(jax.random.fold_in(jax.random.fold_in(rng, 6), position), (shards_of,), jnp.float32, least / len(cuts), top_value / len(cuts))
        return jnp.repeat(jnp.exp(steps), dims[position] // shards_of).reshape((-1,) + (1,) * (len(dims) - position - 1))

    loudness = one(*cuts[0])
    for cut in cuts[1:]:
        loudness = loudness * one(*cut)
    return loudness


def scatter_about(own_key, dims, spread, bound, cuts=(), kind=jnp.bfloat16):
    factor_of = shard_levels(own_key, dims, cuts, -0.22, 0.18) if cuts else 1.0
    result = jax.random.normal(own_key, dims, jnp.float32) * spread * factor_of
    return jnp.minimum(jnp.maximum(result, -bound), bound).astype(kind)


def setup_inputs(seed: int = 0) -> dict:
    key_of = jax.random.split(jax.random.key(seed), 6)
    return {
        "src_latent": scatter_about(key_of[0], (DIM, NS), 1.0, 6.0, ((1, 8),)),
        "tgt_latent": scatter_about(key_of[1], (DIM, NT), 1.0, 6.0, ((1, 4),)),
        "g_start": scatter_about(key_of[2], (NT,), 0.25, 1.5, ((0, 4),), jnp.float32),
        "pairs": draw_pairs(jax.random.fold_in(key_of[5], 71), 0),
        "counts": draw_counts(jax.random.fold_in(key_of[5], 71), 0),
    }


epsilon = 0.01
very_low = -1e30


def tile_score(src_latent, tgt_latent, sq_src, sq_tgt, s_off, t_off, row_pot, col_pot):
    xs = lax.dynamic_slice_in_dim(src_latent, s_off, BLOCK, 1)
    ys = lax.dynamic_slice_in_dim(tgt_latent, t_off, BLOCK, 1)
    cross = lax.dot_general(xs, ys, (((0,), (0,)), ((), ())), preferred_element_type=jnp.float32)
    sx = lax.dynamic_slice_in_dim(sq_src, s_off, BLOCK)
    sy = lax.dynamic_slice_in_dim(sq_tgt, t_off, BLOCK)
    cost = (sx[:, None] + sy[None, :] - 2.0 * cross) / DIM
    shifted = -cost
    if row_pot is not None:
        shifted = shifted + lax.dynamic_slice_in_dim(row_pot, s_off, BLOCK)[:, None]
    if col_pot is not None:
        shifted = shifted + lax.dynamic_slice_in_dim(col_pot, t_off, BLOCK)[None, :]
    return shifted / epsilon, ys


def reference(src_latent, tgt_latent, g_start, pairs, counts):
    sq_src = jnp.sum(jnp.square(src_latent.astype(jnp.float32)), axis=0)
    sq_tgt = jnp.sum(jnp.square(tgt_latent.astype(jnp.float32)), axis=0)
    rr = jnp.arange(N_ROW, dtype=jnp.int32)[:, None, None]
    cc = jnp.arange(N_COL, dtype=jnp.int32)[None, :, None]
    pp = jnp.arange(PAIRS, dtype=jnp.int32)[None, None, :]
    s_offs = ((rr * SB + pairs[..., 0]) * BLOCK).reshape(-1).astype(jnp.int32)
    t_offs = ((cc * TB + pairs[..., 1]) * BLOCK).reshape(-1).astype(jnp.int32)
    live = (pp < counts[:, :, None]).reshape(-1)
    items = (s_offs, t_offs, live)

    def score_of(s_off, t_off, row_pot, col_pot):
        return tile_score(src_latent, tgt_latent, sq_src, sq_tgt, s_off, t_off, row_pot, col_pot)

    def peaks(row_pot, col_pot, axis, length):
        def step(peak, item):
            s_off, t_off, valid = item
            score, _ = score_of(s_off, t_off, row_pot, col_pot)
            off = s_off if axis == 1 else t_off
            red = jnp.where(valid, jnp.max(score, axis=axis), very_low)
            old = lax.dynamic_slice_in_dim(peak, off, BLOCK)
            return lax.dynamic_update_slice_in_dim(peak, jnp.maximum(old, red), off, 0), None
        return lax.scan(step, jnp.full((length,), very_low, jnp.float32), items)[0]

    def totals(row_pot, col_pot, axis, length, peak):
        def step(total, item):
            s_off, t_off, valid = item
            score, _ = score_of(s_off, t_off, row_pot, col_pot)
            off = s_off if axis == 1 else t_off
            pk = lax.dynamic_slice_in_dim(peak, off, BLOCK)
            pk = pk[:, None] if axis == 1 else pk[None, :]
            red = jnp.where(valid, jnp.sum(jnp.exp(score - pk), axis=axis), 0.0)
            old = lax.dynamic_slice_in_dim(total, off, BLOCK)
            return lax.dynamic_update_slice_in_dim(total, old + red, off, 0), None
        return lax.scan(step, jnp.zeros((length,), jnp.float32), items)[0]

    peak_f = peaks(None, g_start, 1, NS)
    total_f = totals(None, g_start, 1, NS, peak_f)
    f_new = -epsilon * jnp.log(1.0 * NS) - epsilon * (peak_f + jnp.log(total_f))
    peak_g = peaks(f_new, None, 0, NT)
    total_g = totals(f_new, None, 0, NT, peak_g)
    g_new = -epsilon * jnp.log(1.0 * NT) - epsilon * (peak_g + jnp.log(total_g))
    peak_b = peaks(None, g_new, 1, NS)

    def step(carry, item):
        numer, denom = carry
        s_off, t_off, valid = item
        score, ys = score_of(s_off, t_off, None, g_new)
        pk = lax.dynamic_slice_in_dim(peak_b, s_off, BLOCK)
        weight = jnp.where(valid, jnp.exp(score - pk[:, None]), 0.0).astype(jnp.bfloat16)
        part = lax.dot_general(ys, weight, (((1,), (1,)), ((), ())), preferred_element_type=jnp.float32)
        old = lax.dynamic_slice_in_dim(numer, s_off, BLOCK, 1)
        numer = lax.dynamic_update_slice_in_dim(numer, old + part, s_off, 1)
        oldd = lax.dynamic_slice_in_dim(denom, s_off, BLOCK)
        denom = lax.dynamic_update_slice_in_dim(denom, oldd + jnp.sum(weight.astype(jnp.float32), axis=1), s_off, 0)
        return (numer, denom), None

    init = (jnp.zeros((DIM, NS), jnp.float32), jnp.zeros((NS,), jnp.float32))
    numer, denom = lax.scan(step, init, items)[0]
    bary = numer / denom[None, :]
    return f_new, g_new, bary
```

```python
import functools
import math

import jax
import jax.numpy as jnp
from jax import lax
from jax.experimental import pallas as pl
from jax.experimental.pallas import tpu as pltpu
from jax.sharding import PartitionSpec as P

BLOCK = 512
HALF = 256
EXTRA = 16

epsilon = 0.01
very_low = -1e30
log2e = 1.0 / math.log(2.0)
MESH = pl.DeviceIdType.MESH


def dot(a, b, a_dim, b_dim):
    return lax.dot_general(
        a, b, (((a_dim,), (b_dim,)), ((), ())), preferred_element_type=jnp.float32
    )


def three(v):
    hi = v.astype(jnp.bfloat16).astype(jnp.float32)
    rest = v - hi
    mid = rest.astype(jnp.bfloat16).astype(jnp.float32)
    return hi, mid, rest - mid


def tail(first, second):
    row = lax.broadcasted_iota(jnp.int32, (EXTRA, BLOCK), 0)
    out = jnp.zeros((EXTRA, BLOCK), jnp.float32)
    for start, value in ((0, first), (3, second)):
        for k in range(3):
            part = value[k] if isinstance(value, tuple) else value
            out = jnp.where(row == start + k, part, out)
    return out.astype(jnp.bfloat16)


def scaled_rows(x, scale):
    return [part.astype(jnp.bfloat16) for part in three(x.astype(jnp.float32) * scale)]


def column_lse(lhs, rhs):
    out = []
    for h in range(BLOCK // HALF):
        score = dot(lhs, rhs[:, h * HALF : (h + 1) * HALF], 0, 0)
        top = jnp.max(score, axis=0, keepdims=True)
        total = jnp.sum(jnp.exp2(score - top), axis=0, keepdims=True)
        out.append(top + jnp.log(total) * log2e)
    return jnp.concatenate(out, axis=1)


def merge_slots(lse, ids, block):
    own = ids == block
    top = jnp.max(jnp.where(own, lse, very_low), axis=0, keepdims=True)
    total = jnp.sum(jnp.where(own, jnp.exp2(lse - top), 0.0), axis=0, keepdims=True)
    return jnp.where(total > 0.0, top + jnp.log(jnp.maximum(total, 1e-30)) * log2e, very_low)


def merge_devices(ref, n):
    top = lax.fori_loop(1, n, lambda c, t: jnp.maximum(t, ref[c]), ref[0])
    total = lax.fori_loop(
        0, n, lambda c, t: t + jnp.exp2(ref[c] - top), jnp.zeros(top.shape, jnp.float32)
    )
    return top + jnp.log(total) * log2e


def potentials_kernel(
    n_row, n_col, sb, tb, slots, width,
    x_ref, y_ref, g_ref, pairs_ref, counts_ref,
    lse_f_ref, all_g_ref, all_y_ref, all_meta_ref,
    x_aug, y_aug, y_wide, slot_lse, from_col, from_row, meta,
    meta_send, meta_recv, f_send, f_recv, g_send, g_recv, h_send, h_recv,
    y_send, y_recv, z_send, z_recv, local_sem,
):
    row = lax.axis_index("row")
    col = lax.axis_index("col")
    core = lax.rem(row, 2)
    sibling = row + 1 - 2 * core
    half = width // 2
    deep = 3 * width

    barrier = pltpu.get_barrier_semaphore()

    def over(n, me, do):
        def step(d, carry):
            do(lax.rem(me + d, n))
            return carry

        lax.fori_loop(1, n, step, 0)

    over(n_col, col, lambda c: pl.semaphore_signal(
        barrier, inc=1, device_id=(row, c), device_id_type=MESH))
    over(n_row, row, lambda r: pl.semaphore_signal(
        barrier, inc=1, device_id=(r, col), device_id_type=MESH))

    def to_col(src, dst, send, recv, c):
        return pltpu.make_async_remote_copy(
            src_ref=src, dst_ref=dst.at[col], send_sem=send.at[c], recv_sem=recv.at[col],
            device_id=(row, c), device_id_type=MESH)

    def from_col_of(dst, send, recv, c):
        return pltpu.make_async_remote_copy(
            src_ref=dst.at[c], dst_ref=dst.at[c], send_sem=send.at[c], recv_sem=recv.at[c],
            device_id=(row, c), device_id_type=MESH)

    count = counts_ref[0, 0]
    lane = lax.broadcasted_iota(jnp.int32, (1, 128), 1)
    slot = lax.broadcasted_iota(jnp.int32, (slots, BLOCK), 0)
    ids_s = jnp.full((slots, BLOCK), -1, jnp.int32)
    ids_t = jnp.full((slots, BLOCK), -1, jnp.int32)
    packed = jnp.where(lane == 2 * slots, count, 0)
    for p in range(slots):
        ids_s = jnp.where(slot == p, pairs_ref[0, 0, p, 0], ids_s)
        ids_t = jnp.where(slot == p, pairs_ref[0, 0, p, 1], ids_t)
        packed = jnp.where(lane == 2 * p, pairs_ref[0, 0, p, 0], packed)
        packed = jnp.where(lane == 2 * p + 1, pairs_ref[0, 0, p, 1], packed)
    ids_s = jnp.where(slot < count, ids_s, -1)
    ids_t = jnp.where(slot < count, ids_t, -1)
    meta[...] = packed

    def prepare_x(s, carry):
        off = pl.multiple_of(s * BLOCK, BLOCK)
        x = x_ref[:, pl.ds(off, BLOCK)]
        for k, part in enumerate(scaled_rows(x, 2.0 * log2e / (width * epsilon))):
            x_aug[s, k * width : (k + 1) * width, :] = part
        x_aug[s, deep : deep + EXTRA, :] = tail(0.0, 1.0)
        return carry

    def prepare_y(t, carry):
        off = pl.multiple_of(t * BLOCK, BLOCK)
        y = y_ref[:, pl.ds(off, BLOCK)]
        yf = y.astype(jnp.float32)
        y_wide[:, pl.ds(off, BLOCK)] = yf
        for k in range(3):
            y_aug[t, k * width : (k + 1) * width, :] = y
        sq = jnp.sum(yf * yf, axis=0, keepdims=True)
        v = (g_ref[:, pl.ds(off, BLOCK)] - sq * (1.0 / width)) * (log2e / epsilon)
        y_aug[t, deep : deep + EXTRA, :] = tail(1.0, three(v))
        return carry

    lax.fori_loop(0, sb, prepare_x, 0)
    lax.fori_loop(0, tb, prepare_y, 0)

    local_y = pltpu.make_async_copy(y_wide, all_y_ref.at[col], local_sem.at[0])
    local_y.start()
    local_meta = pltpu.make_async_copy(meta, all_meta_ref.at[col], local_sem.at[1])
    local_meta.start()

    def source_step(p, carry):
        slot_lse[pl.ds(p, 1), :] = column_lse(
            y_aug[pairs_ref[0, 0, p, 1]], x_aug[pairs_ref[0, 0, p, 0]])
        return carry

    lax.fori_loop(0, slots, source_step, 0)
    lse = slot_lse[...]
    for s in range(sb):
        lse_f_ref[s : s + 1, :] = merge_slots(lse, ids_s, s)
    from_col[col] = lse_f_ref[...]

    pl.semaphore_wait(barrier, n_col + n_row - 2)
    over(n_col, col, lambda c: to_col(lse_f_ref, from_col, f_send, f_recv, c).start())
    over(n_col, col, lambda c: to_col(meta, all_meta_ref, meta_send, meta_recv, c).start())
    over(n_col, col, lambda c: from_col_of(from_col, f_send, f_recv, c).wait_recv())

    own_half = pl.ds(pl.multiple_of(core * half, half), half)
    other_half = pl.ds(pl.multiple_of((1 - core) * half, half), half)

    def y_copy(source, c):
        return pltpu.make_async_remote_copy(
            src_ref=y_wide.at[own_half], dst_ref=all_y_ref.at[source, own_half],
            send_sem=y_send.at[c], recv_sem=y_recv.at[source],
            device_id=(row, c), device_id_type=MESH)

    over(n_col, col, lambda c: y_copy(col, c).start())
    over(n_col, col, lambda c: to_col(lse_f_ref, from_col, f_send, f_recv, c).wait_send())

    merged = merge_devices(from_col, n_col)
    lse_f_ref[...] = merged
    for s in range(sb):
        u = -math.log2(sb * BLOCK * n_row) - merged[s : s + 1, :]
        x_aug[s, deep : deep + EXTRA, :] = tail(three(u), 0.0)

    def target_step(p, carry):
        slot_lse[pl.ds(p, 1), :] = column_lse(
            x_aug[pairs_ref[0, 0, p, 0]], y_aug[pairs_ref[0, 0, p, 1]])
        return carry

    lax.fori_loop(0, slots, target_step, 0)
    lse = slot_lse[...]
    for t in range(tb):
        from_row[row, t : t + 1, :] = merge_slots(lse, ids_t, t)

    def g_copy(source, r):
        return pltpu.make_async_remote_copy(
            src_ref=from_row.at[source], dst_ref=from_row.at[source],
            send_sem=g_send.at[r], recv_sem=g_recv.at[source],
            device_id=(r, col), device_id_type=MESH)

    over(n_row, row, lambda r: g_copy(row, r).start())
    over(n_row, row, lambda r: g_copy(r, r).wait_recv())
    all_g_ref[col] = merge_devices(from_row, n_row)

    def h_copy(source, c):
        return pltpu.make_async_remote_copy(
            src_ref=all_g_ref.at[source], dst_ref=all_g_ref.at[source],
            send_sem=h_send.at[c], recv_sem=h_recv.at[source],
            device_id=(row, c), device_id_type=MESH)

    over(n_col, col, lambda c: h_copy(col, c).start())

    def z_copy(source, part):
        return pltpu.make_async_remote_copy(
            src_ref=all_y_ref.at[source, part], dst_ref=all_y_ref.at[source, part],
            send_sem=z_send.at[source], recv_sem=z_recv.at[source],
            device_id=(sibling, col), device_id_type=MESH)

    def forward(c):
        y_copy(c, c).wait_recv()
        z_copy(c, own_half).start()

    over(n_col, col, forward)
    over(n_col, col, lambda c: h_copy(c, c).wait_recv())
    over(n_col, col, lambda c: from_col_of(all_meta_ref, meta_send, meta_recv, c).wait_recv())
    over(n_col, col, lambda c: z_copy(c, other_half).wait_recv())
    over(n_col, col, lambda c: z_copy(c, own_half).wait_send())
    over(n_col, col, lambda c: y_copy(col, c).wait_send())
    over(n_col, col, lambda c: to_col(meta, all_meta_ref, meta_send, meta_recv, c).wait_send())
    over(n_col, col, lambda c: h_copy(col, c).wait_send())
    over(n_row, row, lambda r: g_copy(row, r).wait_send())
    local_y.wait()
    local_meta.wait()


def map_kernel(
    n_row, n_col, sb, tb, slots, width,
    meta_ref, x_ref, y_ref, lse_f_ref, all_g_ref, all_y_ref,
    f_ref, g_ref, bary_ref,
    x_aug, acc, peak,
):
    deep = 3 * width
    col = lax.axis_index("col")
    log_ns = math.log(sb * BLOCK * n_row)
    log_nt = math.log(tb * BLOCK * n_col)

    def prepare(s, carry):
        off = pl.multiple_of(s * BLOCK, BLOCK)
        x = x_ref[:, pl.ds(off, BLOCK)]
        for k, part in enumerate(scaled_rows(x, 2.0 * log2e / (width * epsilon))):
            x_aug[s, k * width : (k + 1) * width, :] = part
        x_aug[s, deep : deep + EXTRA, :] = tail(0.0, 1.0)
        xf = x.astype(jnp.float32)
        sq = jnp.sum(xf * xf, axis=0, keepdims=True)
        lse = lse_f_ref[pl.ds(s, 1), :]
        f_ref[:, pl.ds(off, BLOCK)] = sq * (1.0 / width) - epsilon * (log_ns + lse / log2e)
        return carry

    lax.fori_loop(0, sb, prepare, 0)
    acc[...] = jnp.zeros_like(acc)
    peak[...] = jnp.full(peak.shape, very_low, jnp.float32)

    def finish_g(t, carry):
        off = pl.multiple_of(t * BLOCK, BLOCK)
        yf = y_ref[:, pl.ds(off, BLOCK)].astype(jnp.float32)
        sq = jnp.sum(yf * yf, axis=0, keepdims=True)
        lse = all_g_ref[col, pl.ds(t, 1), :]
        g_ref[:, pl.ds(off, BLOCK)] = sq * (1.0 / width) - epsilon * (log_nt + lse / log2e)
        return carry

    lax.fori_loop(0, tb, finish_g, 0)

    def column(c, carry):
        def tile(p, carry):
            s = meta_ref[c, 0, 2 * p]
            t = meta_ref[c, 0, 2 * p + 1]
            off = pl.multiple_of(t * BLOCK, BLOCK)
            y = all_y_ref[c, :, pl.ds(off, BLOCK)].astype(jnp.bfloat16)
            w = -all_g_ref[c, pl.ds(t, 1), :]
            lhs = jnp.concatenate([y, y, y, tail(0.0, three(w))], axis=0)
            sums = jnp.concatenate([y, jnp.ones((EXTRA, BLOCK), jnp.bfloat16)], axis=0)
            for h in range(BLOCK // HALF):
                at = slice(h * HALF, (h + 1) * HALF)
                score = dot(lhs, x_aug[s, :, at], 0, 0)
                old = peak[s, :, at]
                top = jnp.maximum(old, jnp.max(score, axis=0, keepdims=True))
                weight = jnp.exp2(score - top).astype(jnp.bfloat16)
                part = dot(sums, weight, 1, 0)
                acc[s, :, at] = acc[s, :, at] * jnp.exp2(old - top) + part
                peak[s, :, at] = top
            return carry

        return lax.fori_loop(0, meta_ref[c, 0, 2 * slots], tile, carry)

    lax.fori_loop(0, n_col, column, 0)

    def finish(s, carry):
        off = pl.multiple_of(s * BLOCK, BLOCK)
        bary_ref[:, pl.ds(off, BLOCK)] = acc[s, :width, :] / acc[s, width : width + 1, :]
        return carry

    lax.fori_loop(0, sb, finish, 0)


def body(n_row, n_col, src_latent, tgt_latent, g_start, pairs, counts):
    width, src_len = src_latent.shape
    tgt_len = tgt_latent.shape[1]
    slots = pairs.shape[2]
    sb, tb = src_len // BLOCK, tgt_len // BLOCK
    rows = 3 * width + EXTRA
    sizes = (n_row, n_col, sb, tb, slots, width)
    vmem = pl.BlockSpec(memory_space=pltpu.VMEM)
    smem = pl.BlockSpec(memory_space=pltpu.SMEM)
    anywhere = pl.BlockSpec(memory_space=pl.ANY)
    limit = pltpu.CompilerParams
    f32 = jnp.float32
    sem = pltpu.SemaphoreType.DMA

    lse_f, all_g, all_y, all_meta = pl.pallas_call(
        functools.partial(potentials_kernel, *sizes),
        out_shape=(
            jax.ShapeDtypeStruct((sb, BLOCK), f32),
            jax.ShapeDtypeStruct((n_col, tb, BLOCK), f32),
            jax.ShapeDtypeStruct((n_col, width, tgt_len), f32),
            jax.ShapeDtypeStruct((n_col, 1, 128), jnp.int32),
        ),
        in_specs=[vmem, vmem, vmem, smem, smem],
        out_specs=(vmem, vmem, anywhere, vmem),
        scratch_shapes=[
            pltpu.VMEM((sb, rows, BLOCK), jnp.bfloat16),
            pltpu.VMEM((tb, rows, BLOCK), jnp.bfloat16),
            pltpu.VMEM((width, tgt_len), f32),
            pltpu.VMEM((slots, BLOCK), f32),
            pltpu.VMEM((n_col, sb, BLOCK), f32),
            pltpu.VMEM((n_row, tb, BLOCK), f32),
            pltpu.VMEM((1, 128), jnp.int32),
            sem((n_col,)), sem((n_col,)), sem((n_col,)), sem((n_col,)),
            sem((n_row,)), sem((n_row,)), sem((n_col,)), sem((n_col,)),
            sem((n_col,)), sem((n_col,)), sem((n_col,)), sem((n_col,)),
            sem((2,)),
        ],
        compiler_params=limit(
            collective_id=0, has_side_effects=True, vmem_limit_bytes=32 * 2**20
        ),
    )(src_latent, tgt_latent, g_start.reshape(1, tgt_len), pairs, counts)

    f_new, g_new, bary = pl.pallas_call(
        functools.partial(map_kernel, *sizes),
        out_shape=(
            jax.ShapeDtypeStruct((1, src_len), f32),
            jax.ShapeDtypeStruct((1, tgt_len), f32),
            jax.ShapeDtypeStruct((width, src_len), f32),
        ),
        in_specs=[smem, vmem, vmem, vmem, vmem, vmem],
        out_specs=(vmem, vmem, vmem),
        scratch_shapes=[
            pltpu.VMEM((sb, rows, BLOCK), jnp.bfloat16),
            pltpu.VMEM((sb, width + EXTRA, BLOCK), f32),
            pltpu.VMEM((sb, 1, BLOCK), f32),
        ],
        compiler_params=limit(vmem_limit_bytes=40 * 2**20),
    )(all_meta, src_latent, tgt_latent, lse_f, all_g, all_y)
    return (f_new.reshape(src_len), g_new.reshape(tgt_len), bary)


def solution(mesh):
    in_specs = (
        P(None, "row"),
        P(None, "col"),
        P("col"),
        P("row", "col", None, None),
        P("row", "col"),
    )
    out_specs = (P("row"), P("col"), P(None, "row"))
    return jax.shard_map(
        functools.partial(body, mesh.shape["row"], mesh.shape["col"]),
        mesh=mesh, in_specs=in_specs, out_specs=out_specs, check_vma=False,
    )
```

```python
import functools
import math

import jax
import jax.numpy as jnp
from jax import lax
from jax.experimental import pallas as pl
from jax.experimental.pallas import tpu as pltpu
from jax.sharding import PartitionSpec as P

BLOCK = 512
HALF = 256
SUMS = 16
TILES = 2

epsilon = 0.01
very_low = -1e30
log2e = 1.0 / math.log(2.0)
MESH = pl.DeviceIdType.MESH


def dot(a, b, a_dim, b_dim):
    return lax.dot_general(
        a, b, (((a_dim,), (b_dim,)), ((), ())), preferred_element_type=jnp.float32
    )


def three(v):
    hi = v.astype(jnp.bfloat16).astype(jnp.float32)
    rest = v - hi
    mid = rest.astype(jnp.bfloat16).astype(jnp.float32)
    return hi, mid, rest - mid


def tail(rows, first, second):
    row = lax.broadcasted_iota(jnp.int32, (8, BLOCK), 0)
    out = jnp.zeros((8, BLOCK), jnp.float32)
    for start, value in ((0, first), (3, second)):
        if isinstance(value, tuple):
            for k in range(3):
                out = jnp.where(row == start + k, value[k], out)
        elif value:
            out = jnp.where((row >= start) & (row < start + 3), value, out)
    out = jnp.concatenate([out, jnp.zeros((rows - 8, BLOCK), jnp.float32)], axis=0)
    return out.astype(jnp.bfloat16)


def depth_of(width):
    return -(-(3 * width + 16) // 128) * 128


def scaled_rows(x, scale):
    return [part.astype(jnp.bfloat16) for part in three(x.astype(jnp.float32) * scale)]


def column_lse(lhs, rhs):
    out = []
    for h in range(BLOCK // HALF):
        score = dot(lhs, rhs[:, h * HALF : (h + 1) * HALF], 1, 0)
        top = jnp.max(score, axis=0, keepdims=True)
        total = jnp.sum(jnp.exp2(score - top), axis=0, keepdims=True)
        out.append(top + jnp.log(total) * log2e)
    return jnp.concatenate(out, axis=1)


def merge_slots(lse, ids, block):
    own = ids == block
    top = jnp.max(jnp.where(own, lse, very_low), axis=0, keepdims=True)
    total = jnp.sum(jnp.where(own, jnp.exp2(lse - top), 0.0), axis=0, keepdims=True)
    return jnp.where(total > 0.0, top + jnp.log(jnp.maximum(total, 1e-30)) * log2e, very_low)


def merge_devices(ref, n):
    top = lax.fori_loop(1, n, lambda c, t: jnp.maximum(t, ref[c]), ref[0])
    total = lax.fori_loop(
        0, n, lambda c, t: t + jnp.exp2(ref[c] - top), jnp.zeros(top.shape, jnp.float32)
    )
    return top + jnp.log(total) * log2e


def potentials_kernel(
    n_row, n_col, sb, tb, slots, width,
    x_hbm, y_hbm, g_ref, pairs_ref, counts_ref,
    lse_f_ref, all_g_ref, all_y_ref, all_meta_ref,
    x_ref, y_ref, x_aug, y_aug, y_flip, y_wide, slot_lse, from_col, from_row, meta,
    meta_send, meta_recv, f_send, f_recv, g_send, g_recv, h_send, h_recv,
    y_send, y_recv, z_send, z_recv, local_sem,
):
    row = lax.axis_index("row")
    col = lax.axis_index("col")
    core = lax.rem(row, 2)
    sibling = row + 1 - 2 * core
    half = width // 2
    deep = 3 * width
    extra = depth_of(width) - deep

    get_y = pltpu.make_async_copy(y_hbm, y_ref, local_sem.at[2])
    get_y.start()
    get_x = pltpu.make_async_copy(x_hbm, x_ref, local_sem.at[3])
    get_x.start()

    barrier = pltpu.get_barrier_semaphore()

    def over(n, me, do):
        def step(d, carry):
            do(lax.rem(me + d, n))
            return carry

        lax.fori_loop(1, n, step, 0)

    over(n_col, col, lambda c: pl.semaphore_signal(
        barrier, inc=1, device_id=(row, c), device_id_type=MESH))
    over(n_row, row, lambda r: pl.semaphore_signal(
        barrier, inc=1, device_id=(r, col), device_id_type=MESH))

    def to_col(src, dst, send, recv, c):
        return pltpu.make_async_remote_copy(
            src_ref=src, dst_ref=dst.at[col], send_sem=send.at[c], recv_sem=recv.at[col],
            device_id=(row, c), device_id_type=MESH)

    def from_col_of(dst, send, recv, c):
        return pltpu.make_async_remote_copy(
            src_ref=dst.at[c], dst_ref=dst.at[c], send_sem=send.at[c], recv_sem=recv.at[c],
            device_id=(row, c), device_id_type=MESH)

    count = counts_ref[0, 0]
    lane = lax.broadcasted_iota(jnp.int32, (1, 128), 1)
    slot = lax.broadcasted_iota(jnp.int32, (slots, BLOCK), 0)
    ids_s = jnp.full((slots, BLOCK), -1, jnp.int32)
    ids_t = jnp.full((slots, BLOCK), -1, jnp.int32)
    packed = jnp.where(lane == 2 * slots, count, 0)
    for p in range(slots):
        ids_s = jnp.where(slot == p, pairs_ref[0, 0, 0, p], ids_s)
        ids_t = jnp.where(slot == p, pairs_ref[0, 0, 1, p], ids_t)
        packed = jnp.where(lane == 2 * p, pairs_ref[0, 0, 0, p], packed)
        packed = jnp.where(lane == 2 * p + 1, pairs_ref[0, 0, 1, p], packed)
    ids_s = jnp.where(slot < count, ids_s, -1)
    ids_t = jnp.where(slot < count, ids_t, -1)
    meta[...] = packed

    def prepare_x(s, carry):
        off = pl.multiple_of(s * BLOCK, BLOCK)
        x = x_ref[:, pl.ds(off, BLOCK)]
        for k, part in enumerate(scaled_rows(x, 2.0 * log2e / (width * epsilon))):
            x_aug[s, k * width : (k + 1) * width, :] = part
        x_aug[s, deep:, :] = tail(extra, 0.0, 1.0)
        return carry

    def prepare_y(t, carry):
        off = pl.multiple_of(t * BLOCK, BLOCK)
        y = y_ref[:, pl.ds(off, BLOCK)]
        yf = y.astype(jnp.float32)
        y_wide[:, pl.ds(off, BLOCK)] = yf
        for k in range(3):
            y_aug[t, k * width : (k + 1) * width, :] = y
        sq = jnp.sum(yf * yf, axis=0, keepdims=True)
        v = (g_ref[:, pl.ds(off, BLOCK)] - sq * (1.0 / width)) * (log2e / epsilon)
        y_aug[t, deep:, :] = tail(extra, 1.0, three(v))
        y_flip[t] = y_aug[t].T
        return carry

    get_y.wait()
    lax.fori_loop(0, tb, prepare_y, 0)
    get_x.wait()
    lax.fori_loop(0, sb, prepare_x, 0)

    local_y = pltpu.make_async_copy(y_wide, all_y_ref.at[col], local_sem.at[0])
    local_y.start()
    local_meta = pltpu.make_async_copy(meta, all_meta_ref.at[col], local_sem.at[1])
    local_meta.start()

    group = math.gcd(slots, 4)

    def source_step(q, carry):
        for p in [q * group + k for k in range(group)]:
            slot_lse[pl.ds(p, 1), :] = column_lse(
                y_flip[pairs_ref[0, 0, 1, p]], x_aug[pairs_ref[0, 0, 0, p]])
        return carry

    lax.fori_loop(0, slots // group, source_step, 0)
    lse = slot_lse[...]
    for s in range(sb):
        lse_f_ref[s : s + 1, :] = merge_slots(lse, ids_s, s)
    from_col[col] = lse_f_ref[...]

    pl.semaphore_wait(barrier, n_col + n_row - 2)
    over(n_col, col, lambda c: to_col(lse_f_ref, from_col, f_send, f_recv, c).start())
    over(n_col, col, lambda c: to_col(meta, all_meta_ref, meta_send, meta_recv, c).start())
    over(n_col, col, lambda c: from_col_of(from_col, f_send, f_recv, c).wait_recv())

    own_half = pl.ds(pl.multiple_of(core * half, half), half)
    other_half = pl.ds(pl.multiple_of((1 - core) * half, half), half)

    def y_copy(source, c):
        return pltpu.make_async_remote_copy(
            src_ref=y_wide.at[own_half], dst_ref=all_y_ref.at[source, own_half],
            send_sem=y_send.at[c], recv_sem=y_recv.at[source],
            device_id=(row, c), device_id_type=MESH)

    over(n_col, col, lambda c: y_copy(col, c).start())
    over(n_col, col, lambda c: to_col(lse_f_ref, from_col, f_send, f_recv, c).wait_send())

    merged = merge_devices(from_col, n_col)
    lse_f_ref[...] = merged
    for s in range(sb):
        u = -math.log2(sb * BLOCK * n_row) - merged[s : s + 1, :]
        x_aug[s, deep:, :] = tail(extra, three(u), 0.0)

    def target_step(q, carry):
        for p in [q * group + k for k in range(group)]:
            slot_lse[pl.ds(p, 1), :] = column_lse(
                x_aug[pairs_ref[0, 0, 0, p]].T, y_aug[pairs_ref[0, 0, 1, p]])
        return carry

    lax.fori_loop(0, slots // group, target_step, 0)
    lse = slot_lse[...]
    for t in range(tb):
        from_row[row, t : t + 1, :] = merge_slots(lse, ids_t, t)

    def g_copy(source, r):
        return pltpu.make_async_remote_copy(
            src_ref=from_row.at[source], dst_ref=from_row.at[source],
            send_sem=g_send.at[r], recv_sem=g_recv.at[source],
            device_id=(r, col), device_id_type=MESH)

    over(n_row, row, lambda r: g_copy(row, r).start())
    over(n_row, row, lambda r: g_copy(r, r).wait_recv())
    all_g_ref[col] = merge_devices(from_row, n_row)

    def h_copy(source, c):
        return pltpu.make_async_remote_copy(
            src_ref=all_g_ref.at[source], dst_ref=all_g_ref.at[source],
            send_sem=h_send.at[c], recv_sem=h_recv.at[source],
            device_id=(row, c), device_id_type=MESH)

    over(n_col, col, lambda c: h_copy(col, c).start())

    def z_copy(source, part):
        return pltpu.make_async_remote_copy(
            src_ref=all_y_ref.at[source, part], dst_ref=all_y_ref.at[source, part],
            send_sem=z_send.at[source], recv_sem=z_recv.at[source],
            device_id=(sibling, col), device_id_type=MESH)

    def forward(c):
        y_copy(c, c).wait_recv()
        z_copy(c, own_half).start()

    over(n_col, col, forward)
    over(n_col, col, lambda c: h_copy(c, c).wait_recv())
    over(n_col, col, lambda c: from_col_of(all_meta_ref, meta_send, meta_recv, c).wait_recv())
    over(n_col, col, lambda c: z_copy(c, other_half).wait_recv())
    over(n_col, col, lambda c: z_copy(c, own_half).wait_send())
    over(n_col, col, lambda c: y_copy(col, c).wait_send())
    over(n_col, col, lambda c: to_col(meta, all_meta_ref, meta_send, meta_recv, c).wait_send())
    over(n_col, col, lambda c: h_copy(col, c).wait_send())
    over(n_row, row, lambda r: g_copy(row, r).wait_send())
    local_y.wait()
    local_meta.wait()


def map_kernel(
    n_row, n_col, sb, tb, slots, width,
    meta_ref, x_ref, y_ref, lse_f_ref, all_g_ref, all_y_ref,
    f_ref, g_ref, bary_ref,
    x_aug, acc, peak, work,
):
    deep = 3 * width
    extra = depth_of(width) - deep
    col = lax.axis_index("col")
    log_ns = math.log(sb * BLOCK * n_row)
    log_nt = math.log(tb * BLOCK * n_col)

    def prepare(s, carry):
        off = pl.multiple_of(s * BLOCK, BLOCK)
        x = x_ref[:, pl.ds(off, BLOCK)]
        for k, part in enumerate(scaled_rows(x, 2.0 * log2e / (width * epsilon))):
            x_aug[s, k * width : (k + 1) * width, :] = part
        x_aug[s, deep:, :] = tail(extra, 0.0, 1.0)
        xf = x.astype(jnp.float32)
        sq = jnp.sum(xf * xf, axis=0, keepdims=True)
        lse = lse_f_ref[pl.ds(s, 1), :]
        f_ref[:, pl.ds(off, BLOCK)] = sq * (1.0 / width) - epsilon * (log_ns + lse / log2e)
        return carry

    lax.fori_loop(0, sb, prepare, 0)
    acc[...] = jnp.zeros_like(acc)
    peak[...] = jnp.full(peak.shape, very_low, jnp.float32)

    def finish_g(t, carry):
        off = pl.multiple_of(t * BLOCK, BLOCK)
        yf = y_ref[:, pl.ds(off, BLOCK)].astype(jnp.float32)
        sq = jnp.sum(yf * yf, axis=0, keepdims=True)
        lse = all_g_ref[col, pl.ds(t, 1), :]
        g_ref[:, pl.ds(off, BLOCK)] = sq * (1.0 / width) - epsilon * (log_nt + lse / log2e)
        return carry

    lax.fori_loop(0, tb, finish_g, 0)

    def list_column(c, at):
        def put(p, at):
            work[0, at] = c
            work[1, at] = meta_ref[c, 0, 2 * p]
            work[2, at] = meta_ref[c, 0, 2 * p + 1]
            return at + 1

        return lax.fori_loop(0, meta_ref[c, 0, 2 * slots], put, at)

    tiles = lax.fori_loop(0, n_col, list_column, 0)

    def tile(n):
        at = jnp.minimum(n, tiles - 1)
        c, s, t = work[0, at], work[1, at], work[2, at]
        off = pl.multiple_of(t * BLOCK, BLOCK)
        y = all_y_ref[c, :, pl.ds(off, BLOCK)].astype(jnp.bfloat16)
        w = -all_g_ref[c, pl.ds(t, 1), :]
        lhs = jnp.concatenate([y, y, y, tail(extra, 0.0, three(w))], axis=0).T
        sums = jnp.concatenate([y, jnp.ones((SUMS, BLOCK), jnp.bfloat16)], axis=0)
        tops, parts = [], []
        for h in range(BLOCK // HALF):
            score = dot(lhs, x_aug[s, :, h * HALF : (h + 1) * HALF], 1, 0)
            top = jnp.max(score, axis=0, keepdims=True)
            weight = jnp.exp2(score - top).astype(jnp.bfloat16)
            parts.append(dot(sums, weight, 1, 0))
            tops.append(top)
        top = jnp.concatenate(tops, axis=1)
        return s, jnp.where(n < tiles, top, very_low), jnp.concatenate(parts, axis=1)

    def step(q, carry):
        done = [tile(q * TILES + k) for k in range(TILES)]
        for s, top, part in done:
            old = peak[s]
            new = jnp.maximum(old, top)
            acc[s] = acc[s] * jnp.exp2(old - new) + part * jnp.exp2(top - new)
            peak[s] = new
        return carry

    lax.fori_loop(0, (tiles + TILES - 1) // TILES, step, 0)

    def finish(s, carry):
        off = pl.multiple_of(s * BLOCK, BLOCK)
        bary_ref[:, pl.ds(off, BLOCK)] = acc[s, :width, :] * (
            1.0 / acc[s, width : width + 1, :])
        return carry

    lax.fori_loop(0, sb, finish, 0)


def body(n_row, n_col, src_latent, tgt_latent, g_start, pairs, counts):
    width, src_len = src_latent.shape
    tgt_len = tgt_latent.shape[1]
    slots = pairs.shape[2]
    sb, tb = src_len // BLOCK, tgt_len // BLOCK
    rows = depth_of(width)
    sizes = (n_row, n_col, sb, tb, slots, width)
    vmem = pl.BlockSpec(memory_space=pltpu.VMEM)
    smem = pl.BlockSpec(memory_space=pltpu.SMEM)
    hbm = pl.BlockSpec(memory_space=pltpu.HBM)
    anywhere = pl.BlockSpec(memory_space=pl.ANY)
    limit = pltpu.CompilerParams
    f32 = jnp.float32
    sem = pltpu.SemaphoreType.DMA

    lse_f, all_g, all_y, all_meta = pl.pallas_call(
        functools.partial(potentials_kernel, *sizes),
        out_shape=(
            jax.ShapeDtypeStruct((sb, BLOCK), f32),
            jax.ShapeDtypeStruct((n_col, tb, BLOCK), f32),
            jax.ShapeDtypeStruct((n_col, width, tgt_len), f32),
            jax.ShapeDtypeStruct((n_col, 1, 128), jnp.int32),
        ),
        in_specs=[hbm, hbm, vmem, smem, smem],
        out_specs=(vmem, vmem, anywhere, vmem),
        scratch_shapes=[
            pltpu.VMEM((width, src_len), jnp.bfloat16),
            pltpu.VMEM((width, tgt_len), jnp.bfloat16),
            pltpu.VMEM((sb, rows, BLOCK), jnp.bfloat16),
            pltpu.VMEM((tb, rows, BLOCK), jnp.bfloat16),
            pltpu.VMEM((tb, BLOCK, rows), jnp.bfloat16),
            pltpu.VMEM((width, tgt_len), f32),
            pltpu.VMEM((slots, BLOCK), f32),
            pltpu.VMEM((n_col, sb, BLOCK), f32),
            pltpu.VMEM((n_row, tb, BLOCK), f32),
            pltpu.VMEM((1, 128), jnp.int32),
            sem((n_col,)), sem((n_col,)), sem((n_col,)), sem((n_col,)),
            sem((n_row,)), sem((n_row,)), sem((n_col,)), sem((n_col,)),
            sem((n_col,)), sem((n_col,)), sem((n_col,)), sem((n_col,)),
            sem((4,)),
        ],
        compiler_params=limit(
            collective_id=0, has_side_effects=True, vmem_limit_bytes=32 * 2**20
        ),
    )(src_latent, tgt_latent, g_start.reshape(1, tgt_len), pairs.transpose(0, 1, 3, 2), counts)

    f_new, g_new, bary = pl.pallas_call(
        functools.partial(map_kernel, *sizes),
        out_shape=(
            jax.ShapeDtypeStruct((1, src_len), f32),
            jax.ShapeDtypeStruct((1, tgt_len), f32),
            jax.ShapeDtypeStruct((width, src_len), f32),
        ),
        in_specs=[smem, vmem, vmem, vmem, vmem, vmem],
        out_specs=(vmem, vmem, vmem),
        scratch_shapes=[
            pltpu.VMEM((sb, rows, BLOCK), jnp.bfloat16),
            pltpu.VMEM((sb, width + SUMS, BLOCK), f32),
            pltpu.VMEM((sb, 1, BLOCK), f32),
            pltpu.SMEM((3, n_col * slots), jnp.int32),
        ],
        compiler_params=limit(vmem_limit_bytes=40 * 2**20),
    )(all_meta, src_latent, tgt_latent, lse_f, all_g, all_y)
    return (f_new.reshape(src_len), g_new.reshape(tgt_len), bary)


def solution(mesh):
    in_specs = (
        P(None, "row"),
        P(None, "col"),
        P("col"),
        P("row", "col", None, None),
        P("row", "col"),
    )
    out_specs = (P("row"), P("col"), P(None, "row"))
    return jax.shard_map(
        functools.partial(body, mesh.shape["row"], mesh.shape["col"]),
        mesh=mesh, in_specs=in_specs, out_specs=out_specs, check_vma=False,
    )
```

```python
import functools
import math

import jax
import jax.numpy as jnp
from jax import lax
from jax.experimental import pallas as pl
from jax.experimental.pallas import tpu as pltpu
from jax.sharding import PartitionSpec as P

BLOCK = 512
HALF = 256
SUMS = 16
TILES = 2

epsilon = 0.01
very_low = -1e30
log2e = 1.0 / math.log(2.0)
MESH = pl.DeviceIdType.MESH


def dot(a, b, a_dim, b_dim):
    return lax.dot_general(
        a, b, (((a_dim,), (b_dim,)), ((), ())), preferred_element_type=jnp.float32
    )


def three(v):
    hi = v.astype(jnp.bfloat16).astype(jnp.float32)
    rest = v - hi
    mid = rest.astype(jnp.bfloat16).astype(jnp.float32)
    return hi, mid, rest - mid


def tail(rows, first, second):
    row = lax.broadcasted_iota(jnp.int32, (8, BLOCK), 0)
    out = jnp.zeros((8, BLOCK), jnp.float32)
    for start, value in ((0, first), (3, second)):
        if isinstance(value, tuple):
            for k in range(3):
                out = jnp.where(row == start + k, value[k], out)
        elif value:
            out = jnp.where((row >= start) & (row < start + 3), value, out)
    out = jnp.concatenate([out, jnp.zeros((rows - 8, BLOCK), jnp.float32)], axis=0)
    return out.astype(jnp.bfloat16)


def depth_of(width):
    return -(-(3 * width + 16) // 128) * 128


def scaled_rows(x, scale):
    return [part.astype(jnp.bfloat16) for part in three(x.astype(jnp.float32) * scale)]


def over_rows(op, x):
    while x.shape[0] > 8:
        ways = 4 if x.shape[0] % 32 == 0 else 2
        n = x.shape[0] // ways
        parts = [x[k * n : (k + 1) * n] for k in range(ways)]
        while len(parts) > 1:
            parts = [op(a, b) for a, b in zip(parts[::2], parts[1::2])]
        x = parts[0]
    return (jnp.max if op is jnp.maximum else jnp.sum)(x, axis=0, keepdims=True)


def column_lse(lhs, rhs):
    out = []
    for h in range(BLOCK // HALF):
        score = dot(lhs, rhs[:, h * HALF : (h + 1) * HALF], 1, 0)
        top = over_rows(jnp.maximum, score)
        total = over_rows(jnp.add, jnp.exp2(score - top))
        out.append(top + jnp.log(total) * log2e)
    return jnp.concatenate(out, axis=1)


def merge_slots(lse, ids, block):
    own = ids == block
    top = jnp.max(jnp.where(own, lse, very_low), axis=0, keepdims=True)
    total = jnp.sum(jnp.where(own, jnp.exp2(lse - top), 0.0), axis=0, keepdims=True)
    return jnp.where(total > 0.0, top + jnp.log(jnp.maximum(total, 1e-30)) * log2e, very_low)


def merge_devices(ref, n):
    top = lax.fori_loop(1, n, lambda c, t: jnp.maximum(t, ref[c]), ref[0])
    total = lax.fori_loop(
        0, n, lambda c, t: t + jnp.exp2(ref[c] - top), jnp.zeros(top.shape, jnp.float32)
    )
    return top + jnp.log(total) * log2e


def potentials_kernel(
    n_row, n_col, sb, tb, slots, width,
    x_hbm, y_hbm, g_hbm, pairs_hbm, counts_ref,
    lse_f_ref, all_g_ref, all_y_ref, all_meta_ref,
    x_ref, y_ref, g_ref, pairs_ref, x_aug, y_aug, y_flip, y_wide, slot_lse, from_col, from_row, meta,
    meta_send, meta_recv, f_send, f_recv, g_send, g_recv, h_send, h_recv,
    y_send, y_recv, z_send, z_recv, local_sem,
):
    row = lax.axis_index("row")
    col = lax.axis_index("col")
    core = lax.rem(row, 2)
    sibling = row + 1 - 2 * core
    half = width // 2
    deep = 3 * width
    extra = depth_of(width) - deep

    get_y = pltpu.make_async_copy(y_hbm, y_ref, local_sem.at[2])
    get_y.start()
    get_x = pltpu.make_async_copy(x_hbm, x_ref, local_sem.at[3])
    get_x.start()

    get_g = pltpu.make_async_copy(g_hbm, g_ref, local_sem.at[4])
    get_g.start()
    get_pairs = pltpu.make_async_copy(pairs_hbm, pairs_ref, local_sem.at[5])
    get_pairs.start()

    barrier = pltpu.get_barrier_semaphore()

    def over(n, me, do):
        def step(d, carry):
            do(lax.rem(me + d, n))
            return carry

        lax.fori_loop(1, n, step, 0)

    over(n_col, col, lambda c: pl.semaphore_signal(
        barrier, inc=1, device_id=(row, c), device_id_type=MESH))
    over(n_row, row, lambda r: pl.semaphore_signal(
        barrier, inc=1, device_id=(r, col), device_id_type=MESH))

    def to_col(src, dst, send, recv, c):
        return pltpu.make_async_remote_copy(
            src_ref=src, dst_ref=dst.at[col], send_sem=send.at[c], recv_sem=recv.at[col],
            device_id=(row, c), device_id_type=MESH)

    def from_col_of(dst, send, recv, c):
        return pltpu.make_async_remote_copy(
            src_ref=dst.at[c], dst_ref=dst.at[c], send_sem=send.at[c], recv_sem=recv.at[c],
            device_id=(row, c), device_id_type=MESH)

    get_pairs.wait()
    count = counts_ref[0, 0]
    lane = lax.broadcasted_iota(jnp.int32, (1, 128), 1)
    slot = lax.broadcasted_iota(jnp.int32, (slots, BLOCK), 0)
    ids_s = jnp.full((slots, BLOCK), -1, jnp.int32)
    ids_t = jnp.full((slots, BLOCK), -1, jnp.int32)
    packed = jnp.where(lane == 2 * slots, count, 0)
    for p in range(slots):
        ids_s = jnp.where(slot == p, pairs_ref[0, 0, 0, p], ids_s)
        ids_t = jnp.where(slot == p, pairs_ref[0, 0, 1, p], ids_t)
        packed = jnp.where(lane == 2 * p, pairs_ref[0, 0, 0, p], packed)
        packed = jnp.where(lane == 2 * p + 1, pairs_ref[0, 0, 1, p], packed)
    ids_s = jnp.where(slot < count, ids_s, -1)
    ids_t = jnp.where(slot < count, ids_t, -1)
    meta[...] = packed

    def prepare_x(s, carry):
        off = pl.multiple_of(s * BLOCK, BLOCK)
        x = x_ref[:, pl.ds(off, BLOCK)]
        for k, part in enumerate(scaled_rows(x, 2.0 * log2e / (width * epsilon))):
            x_aug[s, k * width : (k + 1) * width, :] = part
        x_aug[s, deep:, :] = tail(extra, 0.0, 1.0)
        return carry

    def prepare_y(t, carry):
        off = pl.multiple_of(t * BLOCK, BLOCK)
        y = y_ref[:, pl.ds(off, BLOCK)]
        yf = y.astype(jnp.float32)
        y_wide[:, pl.ds(off, BLOCK)] = yf
        for k in range(3):
            y_aug[t, k * width : (k + 1) * width, :] = y
        sq = jnp.sum(yf * yf, axis=0, keepdims=True)
        v = (g_ref[:, pl.ds(off, BLOCK)] - sq * (1.0 / width)) * (log2e / epsilon)
        y_aug[t, deep:, :] = tail(extra, 1.0, three(v))
        y_flip[t] = y_aug[t].T
        return carry

    get_y.wait()
    get_g.wait()
    lax.fori_loop(0, tb, prepare_y, 0)
    get_x.wait()
    lax.fori_loop(0, sb, prepare_x, 0)

    local_y = pltpu.make_async_copy(y_wide, all_y_ref.at[col], local_sem.at[0])
    local_y.start()
    local_meta = pltpu.make_async_copy(meta, all_meta_ref.at[col], local_sem.at[1])
    local_meta.start()

    group = math.gcd(slots, 4)

    def source_step(q, carry):
        for p in [q * group + k for k in range(group)]:
            slot_lse[pl.ds(p, 1), :] = column_lse(
                y_flip[pairs_ref[0, 0, 1, p]], x_aug[pairs_ref[0, 0, 0, p]])
        return carry

    lax.fori_loop(0, slots // group, source_step, 0)
    lse = slot_lse[...]
    for s in range(sb):
        lse_f_ref[s : s + 1, :] = merge_slots(lse, ids_s, s)
    from_col[col] = lse_f_ref[...]

    pl.semaphore_wait(barrier, n_col + n_row - 2)
    over(n_col, col, lambda c: to_col(lse_f_ref, from_col, f_send, f_recv, c).start())
    over(n_col, col, lambda c: to_col(meta, all_meta_ref, meta_send, meta_recv, c).start())
    over(n_col, col, lambda c: from_col_of(from_col, f_send, f_recv, c).wait_recv())

    own_half = pl.ds(pl.multiple_of(core * half, half), half)
    other_half = pl.ds(pl.multiple_of((1 - core) * half, half), half)

    def y_copy(source, c):
        return pltpu.make_async_remote_copy(
            src_ref=y_wide.at[own_half], dst_ref=all_y_ref.at[source, own_half],
            send_sem=y_send.at[c], recv_sem=y_recv.at[source],
            device_id=(row, c), device_id_type=MESH)

    over(n_col, col, lambda c: y_copy(col, c).start())
    over(n_col, col, lambda c: to_col(lse_f_ref, from_col, f_send, f_recv, c).wait_send())

    merged = merge_devices(from_col, n_col)
    lse_f_ref[...] = merged
    for s in range(sb):
        u = -math.log2(sb * BLOCK * n_row) - merged[s : s + 1, :]
        x_aug[s, deep:, :] = tail(extra, three(u), 0.0)

    def target_step(q, carry):
        for p in [q * group + k for k in range(group)]:
            slot_lse[pl.ds(p, 1), :] = column_lse(
                x_aug[pairs_ref[0, 0, 0, p]].T, y_aug[pairs_ref[0, 0, 1, p]])
        return carry

    lax.fori_loop(0, slots // group, target_step, 0)
    lse = slot_lse[...]
    for t in range(tb):
        from_row[row, t : t + 1, :] = merge_slots(lse, ids_t, t)

    def g_copy(source, r):
        return pltpu.make_async_remote_copy(
            src_ref=from_row.at[source], dst_ref=from_row.at[source],
            send_sem=g_send.at[r], recv_sem=g_recv.at[source],
            device_id=(r, col), device_id_type=MESH)

    over(n_row, row, lambda r: g_copy(row, r).start())
    over(n_row, row, lambda r: g_copy(r, r).wait_recv())
    all_g_ref[col] = merge_devices(from_row, n_row)

    def h_copy(source, c):
        return pltpu.make_async_remote_copy(
            src_ref=all_g_ref.at[source], dst_ref=all_g_ref.at[source],
            send_sem=h_send.at[c], recv_sem=h_recv.at[source],
            device_id=(row, c), device_id_type=MESH)

    over(n_col, col, lambda c: h_copy(col, c).start())

    def z_copy(source, part):
        return pltpu.make_async_remote_copy(
            src_ref=all_y_ref.at[source, part], dst_ref=all_y_ref.at[source, part],
            send_sem=z_send.at[source], recv_sem=z_recv.at[source],
            device_id=(sibling, col), device_id_type=MESH)

    def forward(c):
        y_copy(c, c).wait_recv()
        z_copy(c, own_half).start()

    over(n_col, col, forward)
    over(n_col, col, lambda c: h_copy(c, c).wait_recv())
    over(n_col, col, lambda c: from_col_of(all_meta_ref, meta_send, meta_recv, c).wait_recv())
    over(n_col, col, lambda c: z_copy(c, other_half).wait_recv())
    over(n_col, col, lambda c: z_copy(c, own_half).wait_send())
    over(n_col, col, lambda c: y_copy(col, c).wait_send())
    over(n_col, col, lambda c: to_col(meta, all_meta_ref, meta_send, meta_recv, c).wait_send())
    over(n_col, col, lambda c: h_copy(col, c).wait_send())
    over(n_row, row, lambda r: g_copy(row, r).wait_send())
    local_y.wait()
    local_meta.wait()


def map_kernel(
    n_row, n_col, sb, tb, slots, width,
    meta_ref, x_ref, y_ref, lse_f_ref, all_g_ref, all_y_ref,
    f_ref, g_ref, bary_ref,
    x_aug, acc, peak, work,
):
    deep = 3 * width
    extra = depth_of(width) - deep
    col = lax.axis_index("col")
    log_ns = math.log(sb * BLOCK * n_row)
    log_nt = math.log(tb * BLOCK * n_col)

    def prepare(s, carry):
        off = pl.multiple_of(s * BLOCK, BLOCK)
        x = x_ref[:, pl.ds(off, BLOCK)]
        for k, part in enumerate(scaled_rows(x, 2.0 * log2e / (width * epsilon))):
            x_aug[s, k * width : (k + 1) * width, :] = part
        x_aug[s, deep:, :] = tail(extra, 0.0, 1.0)
        xf = x.astype(jnp.float32)
        sq = jnp.sum(xf * xf, axis=0, keepdims=True)
        lse = lse_f_ref[pl.ds(s, 1), :]
        f_ref[:, pl.ds(off, BLOCK)] = sq * (1.0 / width) - epsilon * (log_ns + lse / log2e)
        return carry

    lax.fori_loop(0, sb, prepare, 0)
    acc[...] = jnp.zeros_like(acc)
    peak[...] = jnp.full(peak.shape, very_low, jnp.float32)

    def finish_g(t, carry):
        off = pl.multiple_of(t * BLOCK, BLOCK)
        yf = y_ref[:, pl.ds(off, BLOCK)].astype(jnp.float32)
        sq = jnp.sum(yf * yf, axis=0, keepdims=True)
        lse = all_g_ref[col, pl.ds(t, 1), :]
        g_ref[:, pl.ds(off, BLOCK)] = sq * (1.0 / width) - epsilon * (log_nt + lse / log2e)
        return carry

    lax.fori_loop(0, tb, finish_g, 0)

    def list_column(c, at):
        def put(p, at):
            work[0, at] = c
            work[1, at] = meta_ref[c, 0, 2 * p]
            work[2, at] = meta_ref[c, 0, 2 * p + 1]
            return at + 1

        return lax.fori_loop(0, meta_ref[c, 0, 2 * slots], put, at)

    tiles = lax.fori_loop(0, n_col, list_column, 0)

    def tile(n):
        at = jnp.minimum(n, tiles - 1)
        c, s, t = work[0, at], work[1, at], work[2, at]
        off = pl.multiple_of(t * BLOCK, BLOCK)
        y = all_y_ref[c, :, pl.ds(off, BLOCK)].astype(jnp.bfloat16)
        w = -all_g_ref[c, pl.ds(t, 1), :]
        lhs = jnp.concatenate([y, y, y, tail(extra, 0.0, three(w))], axis=0).T
        sums = jnp.concatenate([y, jnp.ones((SUMS, BLOCK), jnp.bfloat16)], axis=0)
        tops, parts = [], []
        for h in range(BLOCK // HALF):
            score = dot(lhs, x_aug[s, :, h * HALF : (h + 1) * HALF], 1, 0)
            top = over_rows(jnp.maximum, score)
            weight = jnp.exp2(score - top).astype(jnp.bfloat16)
            parts.append(dot(sums, weight, 1, 0))
            tops.append(top)
        top = jnp.concatenate(tops, axis=1)
        return s, jnp.where(n < tiles, top, very_low), jnp.concatenate(parts, axis=1)

    def step(q, carry):
        done = [tile(q * TILES + k) for k in range(TILES)]
        for s, top, part in done:
            old = peak[s]
            new = jnp.maximum(old, top)
            acc[s] = acc[s] * jnp.exp2(old - new) + part * jnp.exp2(top - new)
            peak[s] = new
        return carry

    lax.fori_loop(0, (tiles + TILES - 1) // TILES, step, 0)

    def finish(s, carry):
        off = pl.multiple_of(s * BLOCK, BLOCK)
        bary_ref[:, pl.ds(off, BLOCK)] = acc[s, :width, :] * (
            1.0 / acc[s, width : width + 1, :])
        return carry

    lax.fori_loop(0, sb, finish, 0)


def in_hbm(x):
    return pltpu.with_memory_space_constraint(x, pltpu.HBM)


def body(n_row, n_col, src_latent, tgt_latent, g_start, pairs, counts):
    width, src_len = src_latent.shape
    tgt_len = tgt_latent.shape[1]
    slots = pairs.shape[2]
    sb, tb = src_len // BLOCK, tgt_len // BLOCK
    rows = depth_of(width)
    sizes = (n_row, n_col, sb, tb, slots, width)
    vmem = pl.BlockSpec(memory_space=pltpu.VMEM)
    smem = pl.BlockSpec(memory_space=pltpu.SMEM)
    hbm = pl.BlockSpec(memory_space=pltpu.HBM)
    anywhere = pl.BlockSpec(memory_space=pl.ANY)
    limit = pltpu.CompilerParams
    f32 = jnp.float32
    sem = pltpu.SemaphoreType.DMA

    lse_f, all_g, all_y, all_meta = pl.pallas_call(
        functools.partial(potentials_kernel, *sizes),
        out_shape=(
            jax.ShapeDtypeStruct((sb, BLOCK), f32),
            jax.ShapeDtypeStruct((n_col, tb, BLOCK), f32),
            jax.ShapeDtypeStruct((n_col, width, tgt_len), f32),
            jax.ShapeDtypeStruct((n_col, 1, 128), jnp.int32),
        ),
        in_specs=[hbm, hbm, hbm, hbm, smem],
        out_specs=(vmem, vmem, anywhere, vmem),
        scratch_shapes=[
            pltpu.VMEM((width, src_len), jnp.bfloat16),
            pltpu.VMEM((width, tgt_len), jnp.bfloat16),
            pltpu.VMEM((1, tgt_len), f32),
            pltpu.SMEM((1, 1, 2, slots), jnp.int32),
            pltpu.VMEM((sb, rows, BLOCK), jnp.bfloat16),
            pltpu.VMEM((tb, rows, BLOCK), jnp.bfloat16),
            pltpu.VMEM((tb, BLOCK, rows), jnp.bfloat16),
            pltpu.VMEM((width, tgt_len), f32),
            pltpu.VMEM((slots, BLOCK), f32),
            pltpu.VMEM((n_col, sb, BLOCK), f32),
            pltpu.VMEM((n_row, tb, BLOCK), f32),
            pltpu.VMEM((1, 128), jnp.int32),
            sem((n_col,)), sem((n_col,)), sem((n_col,)), sem((n_col,)),
            sem((n_row,)), sem((n_row,)), sem((n_col,)), sem((n_col,)),
            sem((n_col,)), sem((n_col,)), sem((n_col,)), sem((n_col,)),
            sem((6,)),
        ],
        compiler_params=limit(
            collective_id=0, has_side_effects=True, vmem_limit_bytes=32 * 2**20
        ),
    )(
        in_hbm(src_latent),
        in_hbm(tgt_latent),
        in_hbm(g_start.reshape(1, tgt_len)),
        in_hbm(pairs.transpose(0, 1, 3, 2)),
        counts,
    )

    f_new, g_new, bary = pl.pallas_call(
        functools.partial(map_kernel, *sizes),
        out_shape=(
            jax.ShapeDtypeStruct((1, src_len), f32),
            jax.ShapeDtypeStruct((1, tgt_len), f32),
            jax.ShapeDtypeStruct((width, src_len), f32),
        ),
        in_specs=[smem, vmem, vmem, vmem, vmem, vmem],
        out_specs=(vmem, vmem, vmem),
        scratch_shapes=[
            pltpu.VMEM((sb, rows, BLOCK), jnp.bfloat16),
            pltpu.VMEM((sb, width + SUMS, BLOCK), f32),
            pltpu.VMEM((sb, 1, BLOCK), f32),
            pltpu.SMEM((3, n_col * slots), jnp.int32),
        ],
        compiler_params=limit(vmem_limit_bytes=40 * 2**20),
    )(all_meta, src_latent, tgt_latent, lse_f, all_g, all_y)
    return (f_new.reshape(src_len), g_new.reshape(tgt_len), bary)


def solution(mesh):
    in_specs = (
        P(None, "row"),
        P(None, "col"),
        P("col"),
        P("row", "col", None, None),
        P("row", "col"),
    )
    out_specs = (P("row"), P("col"), P(None, "row"))
    return jax.shard_map(
        functools.partial(body, mesh.shape["row"], mesh.shape["col"]),
        mesh=mesh, in_specs=in_specs, out_specs=out_specs, check_vma=False,
    )
```

```python
import functools
import math

import jax
import jax.numpy as jnp
from jax import lax
from jax.experimental import pallas as pl
from jax.experimental.pallas import tpu as pltpu
from jax.sharding import PartitionSpec as P

BLOCK = 512
HALF = 256
SUMS = 16
RUN = 64

epsilon = 0.01
very_low = -1e30
log2e = 1.0 / math.log(2.0)
MESH = pl.DeviceIdType.MESH


def dot(a, b, a_dim, b_dim):
    return lax.dot_general(
        a, b, (((a_dim,), (b_dim,)), ((), ())), preferred_element_type=jnp.float32
    )


def three(v):
    hi = v.astype(jnp.bfloat16).astype(jnp.float32)
    rest = v - hi
    mid = rest.astype(jnp.bfloat16).astype(jnp.float32)
    return hi, mid, rest - mid


def tail(rows, first, second):
    row = lax.broadcasted_iota(jnp.int32, (8, BLOCK), 0)
    out = jnp.zeros((8, BLOCK), jnp.float32)
    for start, value in ((0, first), (3, second)):
        if isinstance(value, tuple):
            for k in range(3):
                out = jnp.where(row == start + k, value[k], out)
        elif value:
            out = jnp.where((row >= start) & (row < start + 3), value, out)
    out = jnp.concatenate([out, jnp.zeros((rows - 8, BLOCK), jnp.float32)], axis=0)
    return out.astype(jnp.bfloat16)


def depth_of(width):
    return -(-(3 * width + 16) // 128) * 128


def scaled_rows(x, scale):
    return [part.astype(jnp.bfloat16) for part in three(x.astype(jnp.float32) * scale)]


def over_rows(op, x):
    while x.shape[0] > 8:
        ways = 4 if x.shape[0] % 32 == 0 else 2
        n = x.shape[0] // ways
        parts = [x[k * n : (k + 1) * n] for k in range(ways)]
        while len(parts) > 1:
            parts = [op(a, b) for a, b in zip(parts[::2], parts[1::2])]
        x = parts[0]
    return (jnp.max if op is jnp.maximum else jnp.sum)(x, axis=0, keepdims=True)


def put_scores(buf, lhs, rhs_ref, block):
    for h in range(BLOCK // HALF):
        at = slice(h * HALF, (h + 1) * HALF)
        buf[:, at] = dot(lhs, rhs_ref[block, :, at], 1, 0)


def column_top(buf, at):
    top = buf[0:RUN, at]
    for k in range(RUN, BLOCK, RUN):
        top = jnp.maximum(top, buf[k : k + RUN, at])
    return over_rows(jnp.maximum, top)


def column_lse(buf):
    out = []
    for h in range(BLOCK // HALF):
        at = slice(h * HALF, (h + 1) * HALF)
        top = column_top(buf, at)
        total = jnp.zeros((RUN, HALF), jnp.float32)
        for k in range(0, BLOCK, RUN):
            total = total + jnp.exp2(buf[k : k + RUN, at] - top)
        out.append(top + jnp.log(over_rows(jnp.add, total)) * log2e)
    return jnp.concatenate(out, axis=1)


def merge_slots(lse, ids, block):
    own = ids == block
    top = jnp.max(jnp.where(own, lse, very_low), axis=0, keepdims=True)
    total = jnp.sum(jnp.where(own, jnp.exp2(lse - top), 0.0), axis=0, keepdims=True)
    return jnp.where(total > 0.0, top + jnp.log(jnp.maximum(total, 1e-30)) * log2e, very_low)


def merge_devices(ref, n):
    top = lax.fori_loop(1, n, lambda c, t: jnp.maximum(t, ref[c]), ref[0])
    total = lax.fori_loop(
        0, n, lambda c, t: t + jnp.exp2(ref[c] - top), jnp.zeros(top.shape, jnp.float32)
    )
    return top + jnp.log(total) * log2e


def potentials_kernel(
    n_row, n_col, sb, tb, slots, width,
    x_hbm, y_hbm, g_hbm, pairs_hbm, counts_ref,
    lse_f_ref, all_g_ref, all_y_ref, all_meta_ref,
    x_ref, y_ref, g_ref, pairs_ref, x_aug, y_aug, y_flip, y_wide, slot_lse, from_col, from_row, meta,
    meta_send, meta_recv, f_send, f_recv, g_send, g_recv, h_send, h_recv,
    y_send, y_recv, z_send, z_recv, local_sem, *bufs,
):
    row = lax.axis_index("row")
    col = lax.axis_index("col")
    core = lax.rem(row, 2)
    sibling = row + 1 - 2 * core
    half = width // 2
    deep = 3 * width
    extra = depth_of(width) - deep

    get_y = pltpu.make_async_copy(y_hbm, y_ref, local_sem.at[2])
    get_y.start()
    get_x = pltpu.make_async_copy(x_hbm, x_ref, local_sem.at[3])
    get_x.start()

    get_g = pltpu.make_async_copy(g_hbm, g_ref, local_sem.at[4])
    get_g.start()
    get_pairs = pltpu.make_async_copy(pairs_hbm, pairs_ref, local_sem.at[5])
    get_pairs.start()

    barrier = pltpu.get_barrier_semaphore()

    def over(n, me, do):
        def step(d, carry):
            do(lax.rem(me + d, n))
            return carry

        lax.fori_loop(1, n, step, 0)

    over(n_col, col, lambda c: pl.semaphore_signal(
        barrier, inc=1, device_id=(row, c), device_id_type=MESH))
    over(n_row, row, lambda r: pl.semaphore_signal(
        barrier, inc=1, device_id=(r, col), device_id_type=MESH))

    def to_col(src, dst, send, recv, c):
        return pltpu.make_async_remote_copy(
            src_ref=src, dst_ref=dst.at[col], send_sem=send.at[c], recv_sem=recv.at[col],
            device_id=(row, c), device_id_type=MESH)

    def from_col_of(dst, send, recv, c):
        return pltpu.make_async_remote_copy(
            src_ref=dst.at[c], dst_ref=dst.at[c], send_sem=send.at[c], recv_sem=recv.at[c],
            device_id=(row, c), device_id_type=MESH)

    get_pairs.wait()
    count = counts_ref[0, 0]
    lane = lax.broadcasted_iota(jnp.int32, (1, 128), 1)
    slot = lax.broadcasted_iota(jnp.int32, (slots, BLOCK), 0)
    ids_s = jnp.full((slots, BLOCK), -1, jnp.int32)
    ids_t = jnp.full((slots, BLOCK), -1, jnp.int32)
    packed = jnp.where(lane == 2 * slots, count, 0)
    for p in range(slots):
        ids_s = jnp.where(slot == p, pairs_ref[0, 0, 0, p], ids_s)
        ids_t = jnp.where(slot == p, pairs_ref[0, 0, 1, p], ids_t)
        packed = jnp.where(lane == 2 * p, pairs_ref[0, 0, 0, p], packed)
        packed = jnp.where(lane == 2 * p + 1, pairs_ref[0, 0, 1, p], packed)
    ids_s = jnp.where(slot < count, ids_s, -1)
    ids_t = jnp.where(slot < count, ids_t, -1)
    meta[...] = packed

    def prepare_x(s, carry):
        off = pl.multiple_of(s * BLOCK, BLOCK)
        x = x_ref[:, pl.ds(off, BLOCK)]
        for k, part in enumerate(scaled_rows(x, 2.0 * log2e / (width * epsilon))):
            x_aug[s, k * width : (k + 1) * width, :] = part
        x_aug[s, deep:, :] = tail(extra, 0.0, 1.0)
        return carry

    def prepare_y(t, carry):
        off = pl.multiple_of(t * BLOCK, BLOCK)
        y = y_ref[:, pl.ds(off, BLOCK)]
        yf = y.astype(jnp.float32)
        y_wide[:, pl.ds(off, BLOCK)] = yf
        for k in range(3):
            y_aug[t, k * width : (k + 1) * width, :] = y
        sq = jnp.sum(yf * yf, axis=0, keepdims=True)
        v = (g_ref[:, pl.ds(off, BLOCK)] - sq * (1.0 / width)) * (log2e / epsilon)
        y_aug[t, deep:, :] = tail(extra, 1.0, three(v))
        y_flip[t] = y_aug[t].T
        return carry

    get_y.wait()
    get_g.wait()
    lax.fori_loop(0, tb, prepare_y, 0)
    get_x.wait()
    lax.fori_loop(0, sb, prepare_x, 0)

    local_y = pltpu.make_async_copy(y_wide, all_y_ref.at[col], local_sem.at[0])
    local_y.start()
    local_meta = pltpu.make_async_copy(meta, all_meta_ref.at[col], local_sem.at[1])
    local_meta.start()

    group = math.gcd(slots, 4)

    def in_turn(put, q):
        put(0)
        for k in range(group):
            if k + 1 < group:
                put(k + 1)
            slot_lse[pl.ds(q * group + k, 1), :] = column_lse(bufs[k])

    def source_step(q, carry):
        def put(k):
            p = q * group + k
            put_scores(bufs[k], y_flip[pairs_ref[0, 0, 1, p]], x_aug, pairs_ref[0, 0, 0, p])

        in_turn(put, q)
        return carry

    lax.fori_loop(0, slots // group, source_step, 0)
    lse = slot_lse[...]
    for s in range(sb):
        lse_f_ref[s : s + 1, :] = merge_slots(lse, ids_s, s)
    from_col[col] = lse_f_ref[...]

    pl.semaphore_wait(barrier, n_col + n_row - 2)
    over(n_col, col, lambda c: to_col(lse_f_ref, from_col, f_send, f_recv, c).start())
    over(n_col, col, lambda c: to_col(meta, all_meta_ref, meta_send, meta_recv, c).start())
    over(n_col, col, lambda c: from_col_of(from_col, f_send, f_recv, c).wait_recv())

    own_half = pl.ds(pl.multiple_of(core * half, half), half)
    other_half = pl.ds(pl.multiple_of((1 - core) * half, half), half)

    def y_copy(source, c):
        return pltpu.make_async_remote_copy(
            src_ref=y_wide.at[own_half], dst_ref=all_y_ref.at[source, own_half],
            send_sem=y_send.at[c], recv_sem=y_recv.at[source],
            device_id=(row, c), device_id_type=MESH)

    over(n_col, col, lambda c: y_copy(col, c).start())
    over(n_col, col, lambda c: to_col(lse_f_ref, from_col, f_send, f_recv, c).wait_send())

    merged = merge_devices(from_col, n_col)
    lse_f_ref[...] = merged
    for s in range(sb):
        u = -math.log2(sb * BLOCK * n_row) - merged[s : s + 1, :]
        x_aug[s, deep:, :] = tail(extra, three(u), 0.0)

    def target_step(q, carry):
        def put(k):
            p = q * group + k
            put_scores(bufs[k], x_aug[pairs_ref[0, 0, 0, p]].T, y_aug, pairs_ref[0, 0, 1, p])

        in_turn(put, q)
        return carry

    lax.fori_loop(0, slots // group, target_step, 0)
    lse = slot_lse[...]
    for t in range(tb):
        from_row[row, t : t + 1, :] = merge_slots(lse, ids_t, t)

    def g_copy(source, r):
        return pltpu.make_async_remote_copy(
            src_ref=from_row.at[source], dst_ref=from_row.at[source],
            send_sem=g_send.at[r], recv_sem=g_recv.at[source],
            device_id=(r, col), device_id_type=MESH)

    over(n_row, row, lambda r: g_copy(row, r).start())
    over(n_row, row, lambda r: g_copy(r, r).wait_recv())
    all_g_ref[col] = merge_devices(from_row, n_row)

    def h_copy(source, c):
        return pltpu.make_async_remote_copy(
            src_ref=all_g_ref.at[source], dst_ref=all_g_ref.at[source],
            send_sem=h_send.at[c], recv_sem=h_recv.at[source],
            device_id=(row, c), device_id_type=MESH)

    over(n_col, col, lambda c: h_copy(col, c).start())

    def z_copy(source, part):
        return pltpu.make_async_remote_copy(
            src_ref=all_y_ref.at[source, part], dst_ref=all_y_ref.at[source, part],
            send_sem=z_send.at[source], recv_sem=z_recv.at[source],
            device_id=(sibling, col), device_id_type=MESH)

    def forward(c):
        y_copy(c, c).wait_recv()
        z_copy(c, own_half).start()

    over(n_col, col, forward)
    over(n_col, col, lambda c: h_copy(c, c).wait_recv())
    over(n_col, col, lambda c: from_col_of(all_meta_ref, meta_send, meta_recv, c).wait_recv())
    over(n_col, col, lambda c: z_copy(c, other_half).wait_recv())
    over(n_col, col, lambda c: z_copy(c, own_half).wait_send())
    over(n_col, col, lambda c: y_copy(col, c).wait_send())
    over(n_col, col, lambda c: to_col(meta, all_meta_ref, meta_send, meta_recv, c).wait_send())
    over(n_col, col, lambda c: h_copy(col, c).wait_send())
    over(n_row, row, lambda r: g_copy(row, r).wait_send())
    local_y.wait()
    local_meta.wait()


def map_kernel(
    n_row, n_col, sb, tb, slots, width,
    meta_ref, x_ref, y_ref, lse_f_ref, all_g_ref, all_y_ref,
    f_ref, g_ref, bary_ref,
    x_aug, acc, peak, weights, work, *bufs,
):
    deep = 3 * width
    extra = depth_of(width) - deep
    col = lax.axis_index("col")
    log_ns = math.log(sb * BLOCK * n_row)
    log_nt = math.log(tb * BLOCK * n_col)

    def prepare(s, carry):
        off = pl.multiple_of(s * BLOCK, BLOCK)
        x = x_ref[:, pl.ds(off, BLOCK)]
        for k, part in enumerate(scaled_rows(x, 2.0 * log2e / (width * epsilon))):
            x_aug[s, k * width : (k + 1) * width, :] = part
        x_aug[s, deep:, :] = tail(extra, 0.0, 1.0)
        xf = x.astype(jnp.float32)
        sq = jnp.sum(xf * xf, axis=0, keepdims=True)
        lse = lse_f_ref[pl.ds(s, 1), :]
        f_ref[:, pl.ds(off, BLOCK)] = sq * (1.0 / width) - epsilon * (log_ns + lse / log2e)
        return carry

    lax.fori_loop(0, sb, prepare, 0)
    acc[...] = jnp.zeros_like(acc)
    peak[...] = jnp.full(peak.shape, very_low, jnp.float32)

    def finish_g(t, carry):
        off = pl.multiple_of(t * BLOCK, BLOCK)
        yf = y_ref[:, pl.ds(off, BLOCK)].astype(jnp.float32)
        sq = jnp.sum(yf * yf, axis=0, keepdims=True)
        lse = all_g_ref[col, pl.ds(t, 1), :]
        g_ref[:, pl.ds(off, BLOCK)] = sq * (1.0 / width) - epsilon * (log_nt + lse / log2e)
        return carry

    lax.fori_loop(0, tb, finish_g, 0)

    def list_column(c, at):
        def put(p, at):
            work[0, at] = c
            work[1, at] = meta_ref[c, 0, 2 * p]
            work[2, at] = meta_ref[c, 0, 2 * p + 1]
            return at + 1

        return lax.fori_loop(0, meta_ref[c, 0, 2 * slots], put, at)

    tiles = lax.fori_loop(0, n_col, list_column, 0)

    def place(n):
        at = jnp.minimum(n, tiles - 1)
        return work[0, at], work[1, at], work[2, at]

    def targets(c, t):
        off = pl.multiple_of(t * BLOCK, BLOCK)
        return all_y_ref[c, :, pl.ds(off, BLOCK)].astype(jnp.bfloat16)

    def put(n, buf):
        c, s, t = place(n)
        y = targets(c, t)
        w = -all_g_ref[c, pl.ds(t, 1), :]
        lhs = jnp.concatenate([y, y, y, tail(extra, 0.0, three(w))], axis=0).T
        put_scores(buf, lhs, x_aug, s)

    def use(n, buf):
        c, s, t = place(n)
        sums = jnp.concatenate([targets(c, t), jnp.ones((SUMS, BLOCK), jnp.bfloat16)], axis=0)
        for h in range(BLOCK // HALF):
            at = slice(h * HALF, (h + 1) * HALF)
            top = column_top(buf, at)
            for k in range(0, BLOCK, RUN):
                run = slice(k, k + RUN)
                weights[run, at] = jnp.exp2(buf[run, at] - top).astype(jnp.bfloat16)
            part = dot(sums, weights[:, at], 1, 0)
            top = jnp.where(n < tiles, top, very_low)
            old = peak[s, :, at]
            new = jnp.maximum(old, top)
            acc[s, :, at] = acc[s, :, at] * jnp.exp2(old - new) + part * jnp.exp2(top - new)
            peak[s, :, at] = new

    put(0, bufs[0])

    def step(q, carry):
        put(2 * q + 1, bufs[1])
        use(2 * q, bufs[0])
        put(2 * q + 2, bufs[0])
        use(2 * q + 1, bufs[1])
        return carry

    lax.fori_loop(0, (tiles + 1) // 2, step, 0)

    def finish(s, carry):
        off = pl.multiple_of(s * BLOCK, BLOCK)
        bary_ref[:, pl.ds(off, BLOCK)] = acc[s, :width, :] * (
            1.0 / acc[s, width : width + 1, :])
        return carry

    lax.fori_loop(0, sb, finish, 0)


def in_hbm(x):
    return pltpu.with_memory_space_constraint(x, pltpu.HBM)


def body(n_row, n_col, src_latent, tgt_latent, g_start, pairs, counts):
    width, src_len = src_latent.shape
    tgt_len = tgt_latent.shape[1]
    slots = pairs.shape[2]
    sb, tb = src_len // BLOCK, tgt_len // BLOCK
    rows = depth_of(width)
    sizes = (n_row, n_col, sb, tb, slots, width)
    vmem = pl.BlockSpec(memory_space=pltpu.VMEM)
    smem = pl.BlockSpec(memory_space=pltpu.SMEM)
    hbm = pl.BlockSpec(memory_space=pltpu.HBM)
    anywhere = pl.BlockSpec(memory_space=pl.ANY)
    limit = pltpu.CompilerParams
    f32 = jnp.float32
    sem = pltpu.SemaphoreType.DMA

    lse_f, all_g, all_y, all_meta = pl.pallas_call(
        functools.partial(potentials_kernel, *sizes),
        out_shape=(
            jax.ShapeDtypeStruct((sb, BLOCK), f32),
            jax.ShapeDtypeStruct((n_col, tb, BLOCK), f32),
            jax.ShapeDtypeStruct((n_col, width, tgt_len), f32),
            jax.ShapeDtypeStruct((n_col, 1, 128), jnp.int32),
        ),
        in_specs=[hbm, hbm, hbm, hbm, smem],
        out_specs=(vmem, vmem, anywhere, vmem),
        scratch_shapes=[
            pltpu.VMEM((width, src_len), jnp.bfloat16),
            pltpu.VMEM((width, tgt_len), jnp.bfloat16),
            pltpu.VMEM((1, tgt_len), f32),
            pltpu.SMEM((1, 1, 2, slots), jnp.int32),
            pltpu.VMEM((sb, rows, BLOCK), jnp.bfloat16),
            pltpu.VMEM((tb, rows, BLOCK), jnp.bfloat16),
            pltpu.VMEM((tb, BLOCK, rows), jnp.bfloat16),
            pltpu.VMEM((width, tgt_len), f32),
            pltpu.VMEM((slots, BLOCK), f32),
            pltpu.VMEM((n_col, sb, BLOCK), f32),
            pltpu.VMEM((n_row, tb, BLOCK), f32),
            pltpu.VMEM((1, 128), jnp.int32),
            sem((n_col,)), sem((n_col,)), sem((n_col,)), sem((n_col,)),
            sem((n_row,)), sem((n_row,)), sem((n_col,)), sem((n_col,)),
            sem((n_col,)), sem((n_col,)), sem((n_col,)), sem((n_col,)),
            sem((6,)),
            *[pltpu.VMEM((BLOCK, BLOCK), f32)] * math.gcd(slots, 4),
        ],
        compiler_params=limit(
            collective_id=0, has_side_effects=True, vmem_limit_bytes=32 * 2**20
        ),
    )(
        in_hbm(src_latent),
        in_hbm(tgt_latent),
        in_hbm(g_start.reshape(1, tgt_len)),
        in_hbm(pairs.transpose(0, 1, 3, 2)),
        counts,
    )

    f_new, g_new, bary = pl.pallas_call(
        functools.partial(map_kernel, *sizes),
        out_shape=(
            jax.ShapeDtypeStruct((1, src_len), f32),
            jax.ShapeDtypeStruct((1, tgt_len), f32),
            jax.ShapeDtypeStruct((width, src_len), f32),
        ),
        in_specs=[smem, vmem, vmem, vmem, vmem, vmem],
        out_specs=(vmem, vmem, vmem),
        scratch_shapes=[
            pltpu.VMEM((sb, rows, BLOCK), jnp.bfloat16),
            pltpu.VMEM((sb, width + SUMS, BLOCK), f32),
            pltpu.VMEM((sb, 1, BLOCK), f32),
            pltpu.VMEM((BLOCK, BLOCK), jnp.bfloat16),
            pltpu.SMEM((3, n_col * slots), jnp.int32),
            *[pltpu.VMEM((BLOCK, BLOCK), f32)] * 2,
        ],
        compiler_params=limit(vmem_limit_bytes=40 * 2**20),
    )(all_meta, src_latent, tgt_latent, lse_f, all_g, all_y)
    return (f_new.reshape(src_len), g_new.reshape(tgt_len), bary)


def solution(mesh):
    in_specs = (
        P(None, "row"),
        P(None, "col"),
        P("col"),
        P("row", "col", None, None),
        P("row", "col"),
    )
    out_specs = (P("row"), P("col"), P(None, "row"))
    return jax.shard_map(
        functools.partial(body, mesh.shape["row"], mesh.shape["col"]),
        mesh=mesh, in_specs=in_specs, out_specs=out_specs, check_vma=False,
    )
```

```python
import functools
import math

import jax
import jax.numpy as jnp
from jax import lax
from jax.experimental import pallas as pl
from jax.experimental.pallas import tpu as pltpu
from jax.sharding import PartitionSpec as P

BLOCK = 512
HALF = 256
SUMS = 16
RUN = 64

epsilon = 0.01
very_low = -1e30
log2e = 1.0 / math.log(2.0)
MESH = pl.DeviceIdType.MESH


def dot(a, b, a_dim, b_dim):
    return lax.dot_general(
        a, b, (((a_dim,), (b_dim,)), ((), ())), preferred_element_type=jnp.float32
    )


def three(v):
    hi = v.astype(jnp.bfloat16).astype(jnp.float32)
    rest = v - hi
    mid = rest.astype(jnp.bfloat16).astype(jnp.float32)
    return hi, mid, rest - mid


def tail(rows, first, second):
    row = lax.broadcasted_iota(jnp.int32, (8, BLOCK), 0)
    out = jnp.zeros((8, BLOCK), jnp.float32)
    for start, value in ((0, first), (3, second)):
        if isinstance(value, tuple):
            for k in range(3):
                out = jnp.where(row == start + k, value[k], out)
        elif value:
            out = jnp.where((row >= start) & (row < start + 3), value, out)
    out = jnp.concatenate([out, jnp.zeros((rows - 8, BLOCK), jnp.float32)], axis=0)
    return out.astype(jnp.bfloat16)


def depth_of(width):
    return -(-(3 * width + 16) // 128) * 128


def scaled_rows(x, scale):
    return [part.astype(jnp.bfloat16) for part in three(x.astype(jnp.float32) * scale)]


def over_rows(op, x):
    while x.shape[0] > 8:
        ways = 4 if x.shape[0] % 32 == 0 else 2
        n = x.shape[0] // ways
        parts = [x[k * n : (k + 1) * n] for k in range(ways)]
        while len(parts) > 1:
            parts = [op(a, b) for a, b in zip(parts[::2], parts[1::2])]
        x = parts[0]
    return (jnp.max if op is jnp.maximum else jnp.sum)(x, axis=0, keepdims=True)


def put_scores(buf, lhs, rhs_ref, block):
    for h in range(BLOCK // HALF):
        at = slice(h * HALF, (h + 1) * HALF)
        buf[:, at] = dot(lhs, rhs_ref[block, :, at], 1, 0)


def column_top(buf, at):
    top = buf[0:RUN, at]
    for k in range(RUN, BLOCK, RUN):
        top = jnp.maximum(top, buf[k : k + RUN, at])
    return over_rows(jnp.maximum, top)


def column_lse(buf):
    out = []
    for h in range(BLOCK // HALF):
        at = slice(h * HALF, (h + 1) * HALF)
        top = column_top(buf, at)
        total = jnp.zeros((RUN, HALF), jnp.float32)
        for k in range(0, BLOCK, RUN):
            total = total + jnp.exp2(buf[k : k + RUN, at] - top)
        out.append(top + jnp.log(over_rows(jnp.add, total)) * log2e)
    return jnp.concatenate(out, axis=1)


def merge_slots(lse, ids, block):
    own = ids == block
    top = jnp.max(jnp.where(own, lse, very_low), axis=0, keepdims=True)
    total = jnp.sum(jnp.where(own, jnp.exp2(lse - top), 0.0), axis=0, keepdims=True)
    return jnp.where(total > 0.0, top + jnp.log(jnp.maximum(total, 1e-30)) * log2e, very_low)


def merge_devices(ref, n):
    top = lax.fori_loop(1, n, lambda c, t: jnp.maximum(t, ref[c]), ref[0])
    total = lax.fori_loop(
        0, n, lambda c, t: t + jnp.exp2(ref[c] - top), jnp.zeros(top.shape, jnp.float32)
    )
    return top + jnp.log(total) * log2e


def potentials_kernel(
    n_row, n_col, sb, tb, slots, width,
    x_hbm, y_hbm, g_hbm, pairs_hbm, counts_ref,
    lse_f_ref, all_g_ref, all_y_ref, all_meta_ref,
    x_ref, y_ref, g_ref, pairs_ref, x_aug, y_aug, y_flip, y_wide, slot_lse, from_col, from_row, meta,
    meta_send, meta_recv, f_send, f_recv, g_send, g_recv, h_send, h_recv,
    y_send, y_recv, x_send, x_recv, z_send, z_recv, local_sem, *bufs,
):
    row = lax.axis_index("row")
    col = lax.axis_index("col")
    low = lax.rem(row, 2)
    high = lax.rem(row, 4) // 2
    across = row + 2 - 4 * high
    sibling = row + 1 - 2 * low
    quarter = width // 4

    def rows_of(high, low):
        return pl.ds(pl.multiple_of((2 * high + low) * quarter, quarter), quarter)

    deep = 3 * width
    extra = depth_of(width) - deep

    get_y = pltpu.make_async_copy(y_hbm, y_ref, local_sem.at[2])
    get_y.start()
    get_x = pltpu.make_async_copy(x_hbm, x_ref, local_sem.at[3])
    get_x.start()

    get_g = pltpu.make_async_copy(g_hbm, g_ref, local_sem.at[4])
    get_g.start()
    get_pairs = pltpu.make_async_copy(pairs_hbm, pairs_ref, local_sem.at[5])
    get_pairs.start()

    barrier = pltpu.get_barrier_semaphore()

    def over(n, me, do):
        def step(d, carry):
            do(lax.rem(me + d, n))
            return carry

        lax.fori_loop(1, n, step, 0)

    over(n_col, col, lambda c: pl.semaphore_signal(
        barrier, inc=1, device_id=(row, c), device_id_type=MESH))
    over(n_row, row, lambda r: pl.semaphore_signal(
        barrier, inc=1, device_id=(r, col), device_id_type=MESH))

    def to_col(src, dst, send, recv, c):
        return pltpu.make_async_remote_copy(
            src_ref=src, dst_ref=dst.at[col], send_sem=send.at[c], recv_sem=recv.at[col],
            device_id=(row, c), device_id_type=MESH)

    def from_col_of(dst, send, recv, c):
        return pltpu.make_async_remote_copy(
            src_ref=dst.at[c], dst_ref=dst.at[c], send_sem=send.at[c], recv_sem=recv.at[c],
            device_id=(row, c), device_id_type=MESH)

    get_pairs.wait()
    count = counts_ref[0, 0]
    lane = lax.broadcasted_iota(jnp.int32, (1, 128), 1)
    slot = lax.broadcasted_iota(jnp.int32, (slots, BLOCK), 0)
    ids_s = jnp.full((slots, BLOCK), -1, jnp.int32)
    ids_t = jnp.full((slots, BLOCK), -1, jnp.int32)
    packed = jnp.where(lane == 2 * slots, count, 0)
    for p in range(slots):
        ids_s = jnp.where(slot == p, pairs_ref[0, 0, 0, p], ids_s)
        ids_t = jnp.where(slot == p, pairs_ref[0, 0, 1, p], ids_t)
        packed = jnp.where(lane == 2 * p, pairs_ref[0, 0, 0, p], packed)
        packed = jnp.where(lane == 2 * p + 1, pairs_ref[0, 0, 1, p], packed)
    ids_s = jnp.where(slot < count, ids_s, -1)
    ids_t = jnp.where(slot < count, ids_t, -1)
    meta[...] = packed

    def prepare_x(s, carry):
        off = pl.multiple_of(s * BLOCK, BLOCK)
        x = x_ref[:, pl.ds(off, BLOCK)]
        for k, part in enumerate(scaled_rows(x, 2.0 * log2e / (width * epsilon))):
            x_aug[s, k * width : (k + 1) * width, :] = part
        x_aug[s, deep:, :] = tail(extra, 0.0, 1.0)
        return carry

    def prepare_y(t, carry):
        off = pl.multiple_of(t * BLOCK, BLOCK)
        y = y_ref[:, pl.ds(off, BLOCK)]
        yf = y.astype(jnp.float32)
        y_wide[:, pl.ds(off, BLOCK)] = yf
        for k in range(3):
            y_aug[t, k * width : (k + 1) * width, :] = y
        sq = jnp.sum(yf * yf, axis=0, keepdims=True)
        v = (g_ref[:, pl.ds(off, BLOCK)] - sq * (1.0 / width)) * (log2e / epsilon)
        y_aug[t, deep:, :] = tail(extra, 1.0, three(v))
        y_flip[t] = y_aug[t].T
        return carry

    get_y.wait()
    get_g.wait()
    lax.fori_loop(0, tb, prepare_y, 0)
    def y_copy(source, c):
        return pltpu.make_async_remote_copy(
            src_ref=y_wide.at[rows_of(high, low)],
            dst_ref=all_y_ref.at[source, rows_of(high, low)],
            send_sem=y_send.at[c], recv_sem=y_recv.at[source],
            device_id=(row, c), device_id_type=MESH)

    pl.semaphore_wait(barrier, n_col + n_row - 2)
    over(n_col, col, lambda c: y_copy(col, c).start())
    over(n_col, col, lambda c: to_col(meta, all_meta_ref, meta_send, meta_recv, c).start())

    local_y = pltpu.make_async_copy(y_wide, all_y_ref.at[col], local_sem.at[0])
    local_y.start()
    local_meta = pltpu.make_async_copy(meta, all_meta_ref.at[col], local_sem.at[1])
    local_meta.start()

    get_x.wait()
    lax.fori_loop(0, sb, prepare_x, 0)

    group = math.gcd(slots, 4)

    def in_turn(put, q):
        put(0)
        for k in range(group):
            if k + 1 < group:
                put(k + 1)
            slot_lse[pl.ds(q * group + k, 1), :] = column_lse(bufs[k])

    def source_step(q, carry):
        def put(k):
            p = q * group + k
            put_scores(bufs[k], y_flip[pairs_ref[0, 0, 1, p]], x_aug, pairs_ref[0, 0, 0, p])

        in_turn(put, q)
        return carry

    lax.fori_loop(0, slots // group, source_step, 0)
    lse = slot_lse[...]
    for s in range(sb):
        lse_f_ref[s : s + 1, :] = merge_slots(lse, ids_s, s)
    from_col[col] = lse_f_ref[...]

    over(n_col, col, lambda c: to_col(lse_f_ref, from_col, f_send, f_recv, c).start())
    over(n_col, col, lambda c: from_col_of(from_col, f_send, f_recv, c).wait_recv())

    def x_copy(source, high):
        return pltpu.make_async_remote_copy(
            src_ref=all_y_ref.at[source, rows_of(high, low)],
            dst_ref=all_y_ref.at[source, rows_of(high, low)],
            send_sem=x_send.at[source], recv_sem=x_recv.at[source],
            device_id=(across, col), device_id_type=MESH)

    def pass_across(c):
        y_copy(c, c).wait_recv()
        x_copy(c, high).start()

    over(n_col, col, pass_across)
    over(n_col, col, lambda c: to_col(lse_f_ref, from_col, f_send, f_recv, c).wait_send())

    merged = merge_devices(from_col, n_col)
    lse_f_ref[...] = merged
    for s in range(sb):
        u = -math.log2(sb * BLOCK * n_row) - merged[s : s + 1, :]
        x_aug[s, deep:, :] = tail(extra, three(u), 0.0)

    def target_step(q, carry):
        def put(k):
            p = q * group + k
            put_scores(bufs[k], x_aug[pairs_ref[0, 0, 0, p]].T, y_aug, pairs_ref[0, 0, 1, p])

        in_turn(put, q)
        return carry

    lax.fori_loop(0, slots // group, target_step, 0)
    lse = slot_lse[...]
    for t in range(tb):
        from_row[row, t : t + 1, :] = merge_slots(lse, ids_t, t)

    def g_copy(source, r):
        return pltpu.make_async_remote_copy(
            src_ref=from_row.at[source], dst_ref=from_row.at[source],
            send_sem=g_send.at[r], recv_sem=g_recv.at[source],
            device_id=(r, col), device_id_type=MESH)

    over(n_row, row, lambda r: g_copy(row, r).start())

    def z_copy(source, k, high, low):
        return pltpu.make_async_remote_copy(
            src_ref=all_y_ref.at[source, rows_of(high, low)],
            dst_ref=all_y_ref.at[source, rows_of(high, low)],
            send_sem=z_send.at[k, source], recv_sem=z_recv.at[k, source],
            device_id=(sibling, col), device_id_type=MESH)

    def pass_to_sibling(c):
        x_copy(c, 1 - high).wait_recv()
        z_copy(c, 0, high, low).start()
        z_copy(c, 1, 1 - high, low).start()

    def wait_from_sibling(c):
        z_copy(c, 0, high, 1 - low).wait_recv()
        z_copy(c, 1, 1 - high, 1 - low).wait_recv()

    def wait_to_sibling(c):
        z_copy(c, 0, high, low).wait_send()
        z_copy(c, 1, 1 - high, low).wait_send()

    over(n_col, col, pass_to_sibling)
    over(n_row, row, lambda r: g_copy(r, r).wait_recv())
    all_g_ref[col] = merge_devices(from_row, n_row)

    def h_copy(source, c):
        return pltpu.make_async_remote_copy(
            src_ref=all_g_ref.at[source], dst_ref=all_g_ref.at[source],
            send_sem=h_send.at[c], recv_sem=h_recv.at[source],
            device_id=(row, c), device_id_type=MESH)

    over(n_col, col, lambda c: h_copy(col, c).start())

    over(n_col, col, lambda c: h_copy(c, c).wait_recv())
    over(n_col, col, lambda c: from_col_of(all_meta_ref, meta_send, meta_recv, c).wait_recv())
    over(n_col, col, wait_from_sibling)
    over(n_col, col, wait_to_sibling)
    over(n_col, col, lambda c: x_copy(c, high).wait_send())
    over(n_col, col, lambda c: y_copy(col, c).wait_send())
    over(n_col, col, lambda c: to_col(meta, all_meta_ref, meta_send, meta_recv, c).wait_send())
    over(n_col, col, lambda c: h_copy(col, c).wait_send())
    over(n_row, row, lambda r: g_copy(row, r).wait_send())
    local_y.wait()
    local_meta.wait()


def map_kernel(
    n_row, n_col, sb, tb, slots, width,
    meta_ref, x_ref, y_ref, lse_f_ref, all_g_ref, all_y_ref,
    f_ref, g_ref, bary_ref,
    x_aug, acc, peak, weights, work, *bufs,
):
    deep = 3 * width
    extra = depth_of(width) - deep
    col = lax.axis_index("col")
    log_ns = math.log(sb * BLOCK * n_row)
    log_nt = math.log(tb * BLOCK * n_col)

    def prepare(s, carry):
        off = pl.multiple_of(s * BLOCK, BLOCK)
        x = x_ref[:, pl.ds(off, BLOCK)]
        for k, part in enumerate(scaled_rows(x, 2.0 * log2e / (width * epsilon))):
            x_aug[s, k * width : (k + 1) * width, :] = part
        x_aug[s, deep:, :] = tail(extra, 0.0, 1.0)
        xf = x.astype(jnp.float32)
        sq = jnp.sum(xf * xf, axis=0, keepdims=True)
        lse = lse_f_ref[pl.ds(s, 1), :]
        f_ref[:, pl.ds(off, BLOCK)] = sq * (1.0 / width) - epsilon * (log_ns + lse / log2e)
        return carry

    lax.fori_loop(0, sb, prepare, 0)
    acc[...] = jnp.zeros_like(acc)
    peak[...] = jnp.full(peak.shape, very_low, jnp.float32)

    def finish_g(t, carry):
        off = pl.multiple_of(t * BLOCK, BLOCK)
        yf = y_ref[:, pl.ds(off, BLOCK)].astype(jnp.float32)
        sq = jnp.sum(yf * yf, axis=0, keepdims=True)
        lse = all_g_ref[col, pl.ds(t, 1), :]
        g_ref[:, pl.ds(off, BLOCK)] = sq * (1.0 / width) - epsilon * (log_nt + lse / log2e)
        return carry

    lax.fori_loop(0, tb, finish_g, 0)

    def list_column(c, at):
        def put(p, at):
            work[0, at] = c
            work[1, at] = meta_ref[c, 0, 2 * p]
            work[2, at] = meta_ref[c, 0, 2 * p + 1]
            return at + 1

        return lax.fori_loop(0, meta_ref[c, 0, 2 * slots], put, at)

    tiles = lax.fori_loop(0, n_col, list_column, 0)

    def place(n):
        at = jnp.minimum(n, tiles - 1)
        return work[0, at], work[1, at], work[2, at]

    def targets(c, t):
        off = pl.multiple_of(t * BLOCK, BLOCK)
        return all_y_ref[c, :, pl.ds(off, BLOCK)].astype(jnp.bfloat16)

    def put(n, buf):
        c, s, t = place(n)
        y = targets(c, t)
        w = -all_g_ref[c, pl.ds(t, 1), :]
        lhs = jnp.concatenate([y, y, y, tail(extra, 0.0, three(w))], axis=0).T
        put_scores(buf, lhs, x_aug, s)

    def use(n, buf):
        c, s, t = place(n)
        sums = jnp.concatenate([targets(c, t), jnp.ones((SUMS, BLOCK), jnp.bfloat16)], axis=0)
        for h in range(BLOCK // HALF):
            at = slice(h * HALF, (h + 1) * HALF)
            top = column_top(buf, at)
            for k in range(0, BLOCK, RUN):
                run = slice(k, k + RUN)
                weights[run, at] = jnp.exp2(buf[run, at] - top).astype(jnp.bfloat16)
            part = dot(sums, weights[:, at], 1, 0)
            top = jnp.where(n < tiles, top, very_low)
            old = peak[s, :, at]
            new = jnp.maximum(old, top)
            acc[s, :, at] = acc[s, :, at] * jnp.exp2(old - new) + part * jnp.exp2(top - new)
            peak[s, :, at] = new

    put(0, bufs[0])

    def step(q, carry):
        put(2 * q + 1, bufs[1])
        use(2 * q, bufs[0])
        put(2 * q + 2, bufs[0])
        use(2 * q + 1, bufs[1])
        return carry

    lax.fori_loop(0, (tiles + 1) // 2, step, 0)

    def finish(s, carry):
        off = pl.multiple_of(s * BLOCK, BLOCK)
        bary_ref[:, pl.ds(off, BLOCK)] = acc[s, :width, :] * (
            1.0 / acc[s, width : width + 1, :])
        return carry

    lax.fori_loop(0, sb, finish, 0)


def in_hbm(x):
    return pltpu.with_memory_space_constraint(x, pltpu.HBM)


def body(n_row, n_col, src_latent, tgt_latent, g_start, pairs, counts):
    width, src_len = src_latent.shape
    tgt_len = tgt_latent.shape[1]
    slots = pairs.shape[2]
    sb, tb = src_len // BLOCK, tgt_len // BLOCK
    rows = depth_of(width)
    sizes = (n_row, n_col, sb, tb, slots, width)
    vmem = pl.BlockSpec(memory_space=pltpu.VMEM)
    smem = pl.BlockSpec(memory_space=pltpu.SMEM)
    hbm = pl.BlockSpec(memory_space=pltpu.HBM)
    anywhere = pl.BlockSpec(memory_space=pl.ANY)
    limit = pltpu.CompilerParams
    f32 = jnp.float32
    sem = pltpu.SemaphoreType.DMA

    lse_f, all_g, all_y, all_meta = pl.pallas_call(
        functools.partial(potentials_kernel, *sizes),
        out_shape=(
            jax.ShapeDtypeStruct((sb, BLOCK), f32),
            jax.ShapeDtypeStruct((n_col, tb, BLOCK), f32),
            jax.ShapeDtypeStruct((n_col, width, tgt_len), f32),
            jax.ShapeDtypeStruct((n_col, 1, 128), jnp.int32),
        ),
        in_specs=[hbm, hbm, hbm, hbm, smem],
        out_specs=(vmem, vmem, anywhere, vmem),
        scratch_shapes=[
            pltpu.VMEM((width, src_len), jnp.bfloat16),
            pltpu.VMEM((width, tgt_len), jnp.bfloat16),
            pltpu.VMEM((1, tgt_len), f32),
            pltpu.SMEM((1, 1, 2, slots), jnp.int32),
            pltpu.VMEM((sb, rows, BLOCK), jnp.bfloat16),
            pltpu.VMEM((tb, rows, BLOCK), jnp.bfloat16),
            pltpu.VMEM((tb, BLOCK, rows), jnp.bfloat16),
            pltpu.VMEM((width, tgt_len), f32),
            pltpu.VMEM((slots, BLOCK), f32),
            pltpu.VMEM((n_col, sb, BLOCK), f32),
            pltpu.VMEM((n_row, tb, BLOCK), f32),
            pltpu.VMEM((1, 128), jnp.int32),
            sem((n_col,)), sem((n_col,)), sem((n_col,)), sem((n_col,)),
            sem((n_row,)), sem((n_row,)), sem((n_col,)), sem((n_col,)),
            sem((n_col,)), sem((n_col,)), sem((n_col,)), sem((n_col,)),
            sem((2, n_col)), sem((2, n_col)), sem((6,)),
            *[pltpu.VMEM((BLOCK, BLOCK), f32)] * math.gcd(slots, 4),
        ],
        compiler_params=limit(
            collective_id=0, has_side_effects=True, vmem_limit_bytes=32 * 2**20
        ),
    )(
        in_hbm(src_latent),
        in_hbm(tgt_latent),
        in_hbm(g_start.reshape(1, tgt_len)),
        in_hbm(pairs.transpose(0, 1, 3, 2)),
        counts,
    )

    f_new, g_new, bary = pl.pallas_call(
        functools.partial(map_kernel, *sizes),
        out_shape=(
            jax.ShapeDtypeStruct((1, src_len), f32),
            jax.ShapeDtypeStruct((1, tgt_len), f32),
            jax.ShapeDtypeStruct((width, src_len), f32),
        ),
        in_specs=[smem, vmem, vmem, vmem, vmem, vmem],
        out_specs=(vmem, vmem, vmem),
        scratch_shapes=[
            pltpu.VMEM((sb, rows, BLOCK), jnp.bfloat16),
            pltpu.VMEM((sb, width + SUMS, BLOCK), f32),
            pltpu.VMEM((sb, 1, BLOCK), f32),
            pltpu.VMEM((BLOCK, BLOCK), jnp.bfloat16),
            pltpu.SMEM((3, n_col * slots), jnp.int32),
            *[pltpu.VMEM((BLOCK, BLOCK), f32)] * 2,
        ],
        compiler_params=limit(vmem_limit_bytes=40 * 2**20),
    )(all_meta, src_latent, tgt_latent, lse_f, all_g, all_y)
    return (f_new.reshape(src_len), g_new.reshape(tgt_len), bary)


def solution(mesh):
    in_specs = (
        P(None, "row"),
        P(None, "col"),
        P("col"),
        P("row", "col", None, None),
        P("row", "col"),
    )
    out_specs = (P("row"), P("col"), P(None, "row"))
    return jax.shard_map(
        functools.partial(body, mesh.shape["row"], mesh.shape["col"]),
        mesh=mesh, in_specs=in_specs, out_specs=out_specs, check_vma=False,
    )
```

```python
import functools
import math

import jax
import jax.numpy as jnp
from jax import lax
from jax.experimental import pallas as pl
from jax.experimental.pallas import tpu as pltpu
from jax.sharding import PartitionSpec as P

BLOCK = 512
HALF = 256
SUMS = 16
RUN = 64

epsilon = 0.01
very_low = -1e30
log2e = 1.0 / math.log(2.0)
MESH = pl.DeviceIdType.MESH


def dot(a, b, a_dim, b_dim):
    return lax.dot_general(
        a, b, (((a_dim,), (b_dim,)), ((), ())), preferred_element_type=jnp.float32
    )


def three(v):
    hi = v.astype(jnp.bfloat16).astype(jnp.float32)
    rest = v - hi
    mid = rest.astype(jnp.bfloat16).astype(jnp.float32)
    return hi, mid, rest - mid


def tail(rows, first, second):
    row = lax.broadcasted_iota(jnp.int32, (8, BLOCK), 0)
    out = jnp.zeros((8, BLOCK), jnp.float32)
    for start, value in ((0, first), (3, second)):
        if isinstance(value, tuple):
            for k in range(3):
                out = jnp.where(row == start + k, value[k], out)
        elif value:
            out = jnp.where((row >= start) & (row < start + 3), value, out)
    out = jnp.concatenate([out, jnp.zeros((rows - 8, BLOCK), jnp.float32)], axis=0)
    return out.astype(jnp.bfloat16)


def depth_of(width):
    return -(-(3 * width + 16) // 128) * 128


def scaled_rows(x, scale):
    return [part.astype(jnp.bfloat16) for part in three(x.astype(jnp.float32) * scale)]


def over_rows(op, x):
    while x.shape[0] > 8:
        ways = 4 if x.shape[0] % 32 == 0 else 2
        n = x.shape[0] // ways
        parts = [x[k * n : (k + 1) * n] for k in range(ways)]
        while len(parts) > 1:
            parts = [op(a, b) for a, b in zip(parts[::2], parts[1::2])]
        x = parts[0]
    return (jnp.max if op is jnp.maximum else jnp.sum)(x, axis=0, keepdims=True)


def put_scores(buf, lhs, rhs_ref, block):
    for h in range(BLOCK // HALF):
        at = slice(h * HALF, (h + 1) * HALF)
        buf[:, at] = dot(lhs, rhs_ref[block, :, at], 1, 0)


def column_top(buf, at):
    top = buf[0:RUN, at]
    for k in range(RUN, BLOCK, RUN):
        top = jnp.maximum(top, buf[k : k + RUN, at])
    return over_rows(jnp.maximum, top)


def column_lse(buf):
    out = []
    for h in range(BLOCK // HALF):
        at = slice(h * HALF, (h + 1) * HALF)
        top = column_top(buf, at)
        total = jnp.zeros((RUN, HALF), jnp.float32)
        for k in range(0, BLOCK, RUN):
            total = total + jnp.exp2(buf[k : k + RUN, at] - top)
        out.append(top + jnp.log(over_rows(jnp.add, total)) * log2e)
    return jnp.concatenate(out, axis=1)


def merge_slots(lse, ids, block):
    own = ids == block
    top = jnp.max(jnp.where(own, lse, very_low), axis=0, keepdims=True)
    total = jnp.sum(jnp.where(own, jnp.exp2(lse - top), 0.0), axis=0, keepdims=True)
    return jnp.where(total > 0.0, top + jnp.log(jnp.maximum(total, 1e-30)) * log2e, very_low)


def repeat(n, step, state=None):
    if n > 8:
        return lax.fori_loop(0, n, step, state)
    for k in range(n):
        state = step(k, state)
    return state


def merge_devices(ref, n):
    top = repeat(n, lambda c, t: jnp.maximum(t, ref[c]), ref[0])
    total = repeat(n, lambda c, t: t + jnp.exp2(ref[c] - top), jnp.zeros(top.shape, jnp.float32))
    return top + jnp.log(total) * log2e


def potentials_kernel(
    n_row, n_col, sb, tb, slots, width,
    x_hbm, y_hbm, g_hbm, pairs_hbm, counts_ref,
    f_rows, g_rows, x_aug, all_g_ref, all_y_ref, all_meta_ref,
    x_ref, y_ref, g_ref, pairs_ref, lse_f_ref, sq_x, sq_y, y_aug, y_flip, y_wide, slot_lse, from_col, from_row, meta,
    meta_send, meta_recv, f_send, f_recv, g_send, g_recv, h_send, h_recv,
    y_send, y_recv, x_send, x_recv, z_send, z_recv, local_sem, *bufs,
):
    row = lax.axis_index("row")
    col = lax.axis_index("col")
    low = lax.rem(row, 2)
    high = lax.rem(row, 4) // 2
    across = row + 2 - 4 * high
    sibling = row + 1 - 2 * low
    quarter = width // 4

    def rows_of(high, low):
        return pl.ds(pl.multiple_of((2 * high + low) * quarter, quarter), quarter)

    deep = 3 * width
    extra = depth_of(width) - deep

    get_y = pltpu.make_async_copy(y_hbm, y_ref, local_sem.at[2])
    get_y.start()
    get_x = pltpu.make_async_copy(x_hbm, x_ref, local_sem.at[3])
    get_x.start()

    get_g = pltpu.make_async_copy(g_hbm, g_ref, local_sem.at[4])
    get_g.start()
    get_pairs = pltpu.make_async_copy(pairs_hbm, pairs_ref, local_sem.at[5])
    get_pairs.start()

    barrier = pltpu.get_barrier_semaphore()

    def over(n, me, do):
        def step(d, carry):
            do(lax.rem(me + d, n))
            return carry

        lax.fori_loop(1, n, step, 0)

    over(n_col, col, lambda c: pl.semaphore_signal(
        barrier, inc=1, device_id=(row, c), device_id_type=MESH))
    over(n_row, row, lambda r: pl.semaphore_signal(
        barrier, inc=1, device_id=(r, col), device_id_type=MESH))

    def to_col(src, dst, send, recv, c):
        return pltpu.make_async_remote_copy(
            src_ref=src, dst_ref=dst.at[col], send_sem=send.at[c], recv_sem=recv.at[col],
            device_id=(row, c), device_id_type=MESH)

    def from_col_of(dst, send, recv, c):
        return pltpu.make_async_remote_copy(
            src_ref=dst.at[c], dst_ref=dst.at[c], send_sem=send.at[c], recv_sem=recv.at[c],
            device_id=(row, c), device_id_type=MESH)

    get_pairs.wait()
    count = counts_ref[0, 0]
    lane = lax.broadcasted_iota(jnp.int32, (1, 128), 1)
    slot = lax.broadcasted_iota(jnp.int32, (slots, BLOCK), 0)
    ids_s = jnp.full((slots, BLOCK), -1, jnp.int32)
    ids_t = jnp.full((slots, BLOCK), -1, jnp.int32)
    packed = jnp.where(lane == 2 * slots, count, 0)
    for p in range(slots):
        ids_s = jnp.where(slot == p, pairs_ref[0, 0, 0, p], ids_s)
        ids_t = jnp.where(slot == p, pairs_ref[0, 0, 1, p], ids_t)
        packed = jnp.where(lane == 2 * p, pairs_ref[0, 0, 0, p], packed)
        packed = jnp.where(lane == 2 * p + 1, pairs_ref[0, 0, 1, p], packed)
    ids_s = jnp.where(slot < count, ids_s, -1)
    ids_t = jnp.where(slot < count, ids_t, -1)
    meta[...] = packed

    def prepare_x(s, carry):
        x = x_ref[:, s * BLOCK : (s + 1) * BLOCK]
        for k, part in enumerate(scaled_rows(x, 2.0 * log2e / (width * epsilon))):
            x_aug[s, k * width : (k + 1) * width, :] = part
        x_aug[s, deep:, :] = tail(extra, 0.0, 1.0)
        xf = x.astype(jnp.float32)
        sq_x[s : s + 1, :] = jnp.sum(xf * xf, axis=0, keepdims=True) * (1.0 / width)
        return carry

    def prepare_y(t, carry):
        at = slice(t * BLOCK, (t + 1) * BLOCK)
        y = y_ref[:, at]
        yf = y.astype(jnp.float32)
        y_wide[:, at] = yf
        for k in range(3):
            y_aug[t, k * width : (k + 1) * width, :] = y
        sq = jnp.sum(yf * yf, axis=0, keepdims=True) * (1.0 / width)
        sq_y[t : t + 1, :] = sq
        v = (g_ref[:, at] - sq) * (log2e / epsilon)
        y_aug[t, deep:, :] = tail(extra, 1.0, three(v))
        y_flip[t] = y_aug[t].T
        return carry

    get_y.wait()
    get_g.wait()
    for t in range(tb):
        prepare_y(t, 0)
    get_x.wait()
    for s in range(sb):
        prepare_x(s, 0)

    def y_copy(source, c):
        return pltpu.make_async_remote_copy(
            src_ref=y_wide.at[rows_of(high, low)],
            dst_ref=all_y_ref.at[source, rows_of(high, low)],
            send_sem=y_send.at[c], recv_sem=y_recv.at[source],
            device_id=(row, c), device_id_type=MESH)

    pl.semaphore_wait(barrier, n_col + n_row - 2)
    over(n_col, col, lambda c: y_copy(col, c).start())
    over(n_col, col, lambda c: to_col(meta, all_meta_ref, meta_send, meta_recv, c).start())

    local_y = pltpu.make_async_copy(y_wide, all_y_ref.at[col], local_sem.at[0])
    local_y.start()
    local_meta = pltpu.make_async_copy(meta, all_meta_ref.at[col], local_sem.at[1])
    local_meta.start()

    group = math.gcd(slots, 4)

    def in_turn(put, q):
        put(0)
        for k in range(group):
            if k + 1 < group:
                put(k + 1)
            slot_lse[pl.ds(q * group + k, 1), :] = column_lse(bufs[k])

    def source_step(q, carry):
        def put(k):
            p = q * group + k
            put_scores(bufs[k], y_flip[pairs_ref[0, 0, 1, p]], x_aug, pairs_ref[0, 0, 0, p])

        in_turn(put, q)
        return carry

    lax.fori_loop(0, slots // group, source_step, 0)
    lse = slot_lse[...]
    for s in range(sb):
        lse_f_ref[s : s + 1, :] = merge_slots(lse, ids_s, s)
    from_col[col] = lse_f_ref[...]

    over(n_col, col, lambda c: to_col(lse_f_ref, from_col, f_send, f_recv, c).start())
    over(n_col, col, lambda c: from_col_of(from_col, f_send, f_recv, c).wait_recv())

    def x_copy(source, high):
        return pltpu.make_async_remote_copy(
            src_ref=all_y_ref.at[source, rows_of(high, low)],
            dst_ref=all_y_ref.at[source, rows_of(high, low)],
            send_sem=x_send.at[source], recv_sem=x_recv.at[source],
            device_id=(across, col), device_id_type=MESH)

    def pass_across(c):
        y_copy(c, c).wait_recv()
        x_copy(c, high).start()

    over(n_col, col, pass_across)
    over(n_col, col, lambda c: to_col(lse_f_ref, from_col, f_send, f_recv, c).wait_send())

    merged = merge_devices(from_col, n_col)
    lse_f_ref[...] = merged
    for s in range(sb):
        u = -math.log2(sb * BLOCK * n_row) - merged[s : s + 1, :]
        x_aug[s, deep:, :] = tail(extra, three(u), 0.0)

    def target_step(q, carry):
        def put(k):
            p = q * group + k
            put_scores(bufs[k], x_aug[pairs_ref[0, 0, 0, p]].T, y_aug, pairs_ref[0, 0, 1, p])

        in_turn(put, q)
        return carry

    lax.fori_loop(0, slots // group, target_step, 0)
    lse = slot_lse[...]
    for t in range(tb):
        from_row[row, t : t + 1, :] = merge_slots(lse, ids_t, t)

    def g_copy(source, r):
        return pltpu.make_async_remote_copy(
            src_ref=from_row.at[source], dst_ref=from_row.at[source],
            send_sem=g_send.at[r], recv_sem=g_recv.at[source],
            device_id=(r, col), device_id_type=MESH)

    over(n_row, row, lambda r: g_copy(row, r).start())

    def z_copy(source, k, high, low):
        return pltpu.make_async_remote_copy(
            src_ref=all_y_ref.at[source, rows_of(high, low)],
            dst_ref=all_y_ref.at[source, rows_of(high, low)],
            send_sem=z_send.at[k, source], recv_sem=z_recv.at[k, source],
            device_id=(sibling, col), device_id_type=MESH)

    def pass_to_sibling(c):
        x_copy(c, 1 - high).wait_recv()
        z_copy(c, 0, high, low).start()
        z_copy(c, 1, 1 - high, low).start()

    def wait_from_sibling(c):
        z_copy(c, 0, high, 1 - low).wait_recv()
        z_copy(c, 1, 1 - high, 1 - low).wait_recv()

    def wait_to_sibling(c):
        z_copy(c, 0, high, low).wait_send()
        z_copy(c, 1, 1 - high, low).wait_send()

    over(n_col, col, pass_to_sibling)
    over(n_row, row, lambda r: g_copy(r, r).wait_recv())
    all_g_ref[col] = merge_devices(from_row, n_row)

    def h_copy(source, c):
        return pltpu.make_async_remote_copy(
            src_ref=all_g_ref.at[source], dst_ref=all_g_ref.at[source],
            send_sem=h_send.at[c], recv_sem=h_recv.at[source],
            device_id=(row, c), device_id_type=MESH)

    over(n_col, col, lambda c: h_copy(col, c).start())

    log_ns = math.log(sb * BLOCK * n_row)
    log_nt = math.log(tb * BLOCK * n_col)
    f_rows[...] = sq_x[...] - epsilon * (log_ns + lse_f_ref[...] / log2e)
    g_rows[...] = sq_y[...] - epsilon * (log_nt + all_g_ref[col] / log2e)
    for s in range(sb):
        x_aug[s, deep:, :] = tail(extra, 0.0, 1.0)


    over(n_col, col, lambda c: h_copy(c, c).wait_recv())
    over(n_col, col, lambda c: from_col_of(all_meta_ref, meta_send, meta_recv, c).wait_recv())
    over(n_col, col, wait_from_sibling)
    over(n_col, col, wait_to_sibling)
    over(n_col, col, lambda c: x_copy(c, high).wait_send())
    over(n_col, col, lambda c: y_copy(col, c).wait_send())
    over(n_col, col, lambda c: to_col(meta, all_meta_ref, meta_send, meta_recv, c).wait_send())
    over(n_col, col, lambda c: h_copy(col, c).wait_send())
    over(n_row, row, lambda r: g_copy(row, r).wait_send())
    local_y.wait()
    local_meta.wait()


def map_kernel(
    n_row, n_col, sb, tb, slots, width,
    meta_ref, f_rows, g_rows, x_aug, all_g_ref, all_y_ref,
    f_ref, g_ref, bary_ref,
    acc, peak, weights, work, *bufs,
):
    extra = depth_of(width) - 3 * width
    for rows, out, n in ((f_rows, f_ref, sb), (g_rows, g_ref, tb)):
        for k in range(n):
            out[:, k * BLOCK : (k + 1) * BLOCK] = rows[k : k + 1, :]
    acc[...] = jnp.zeros_like(acc)
    peak[...] = jnp.full(peak.shape, very_low, jnp.float32)

    def list_column(c, at):
        def put(p, at):
            work[0, at] = c
            work[1, at] = meta_ref[c, 0, 2 * p]
            work[2, at] = meta_ref[c, 0, 2 * p + 1]
            return at + 1

        return lax.fori_loop(0, meta_ref[c, 0, 2 * slots], put, at)

    tiles = lax.fori_loop(0, n_col, list_column, 0)

    def place(n):
        at = jnp.minimum(n, tiles - 1)
        return work[0, at], work[1, at], work[2, at]

    def targets(c, t):
        off = pl.multiple_of(t * BLOCK, BLOCK)
        return all_y_ref[c, :, pl.ds(off, BLOCK)].astype(jnp.bfloat16)

    def put(n, buf):
        c, s, t = place(n)
        y = targets(c, t)
        w = -all_g_ref[c, pl.ds(t, 1), :]
        lhs = jnp.concatenate([y, y, y, tail(extra, 0.0, three(w))], axis=0).T
        put_scores(buf, lhs, x_aug, s)

    def use(n, buf):
        c, s, t = place(n)
        sums = jnp.concatenate([targets(c, t), jnp.ones((SUMS, BLOCK), jnp.bfloat16)], axis=0)
        for h in range(BLOCK // HALF):
            at = slice(h * HALF, (h + 1) * HALF)
            top = column_top(buf, at)
            for k in range(0, BLOCK, RUN):
                run = slice(k, k + RUN)
                weights[run, at] = jnp.exp2(buf[run, at] - top).astype(jnp.bfloat16)
            part = dot(sums, weights[:, at], 1, 0)
            top = jnp.where(n < tiles, top, very_low)
            old = peak[s, :, at]
            new = jnp.maximum(old, top)
            acc[s, :, at] = acc[s, :, at] * jnp.exp2(old - new) + part * jnp.exp2(top - new)
            peak[s, :, at] = new

    put(0, bufs[0])

    def step(q, carry):
        put(2 * q + 1, bufs[1])
        use(2 * q, bufs[0])
        put(2 * q + 2, bufs[0])
        use(2 * q + 1, bufs[1])
        return carry

    lax.fori_loop(0, (tiles + 1) // 2, step, 0)

    for s in range(sb):
        bary_ref[:, s * BLOCK : (s + 1) * BLOCK] = acc[s, :width, :] * (
            1.0 / acc[s, width : width + 1, :])


def in_hbm(x):
    return pltpu.with_memory_space_constraint(x, pltpu.HBM)


def body(n_row, n_col, src_latent, tgt_latent, g_start, pairs, counts):
    width, src_len = src_latent.shape
    tgt_len = tgt_latent.shape[1]
    slots = pairs.shape[2]
    sb, tb = src_len // BLOCK, tgt_len // BLOCK
    rows = depth_of(width)
    sizes = (n_row, n_col, sb, tb, slots, width)
    vmem = pl.BlockSpec(memory_space=pltpu.VMEM)
    smem = pl.BlockSpec(memory_space=pltpu.SMEM)
    hbm = pl.BlockSpec(memory_space=pltpu.HBM)
    anywhere = pl.BlockSpec(memory_space=pl.ANY)
    limit = pltpu.CompilerParams
    f32 = jnp.float32
    sem = pltpu.SemaphoreType.DMA

    f_rows, g_rows, x_aug, all_g, all_y, all_meta = pl.pallas_call(
        functools.partial(potentials_kernel, *sizes),
        out_shape=(
            jax.ShapeDtypeStruct((sb, BLOCK), f32),
            jax.ShapeDtypeStruct((tb, BLOCK), f32),
            jax.ShapeDtypeStruct((sb, rows, BLOCK), jnp.bfloat16),
            jax.ShapeDtypeStruct((n_col, tb, BLOCK), f32),
            jax.ShapeDtypeStruct((n_col, width, tgt_len), f32),
            jax.ShapeDtypeStruct((n_col, 1, 128), jnp.int32),
        ),
        in_specs=[hbm, hbm, hbm, hbm, smem],
        out_specs=(vmem, vmem, vmem, vmem, anywhere, vmem),
        scratch_shapes=[
            pltpu.VMEM((width, src_len), jnp.bfloat16),
            pltpu.VMEM((width, tgt_len), jnp.bfloat16),
            pltpu.VMEM((1, tgt_len), f32),
            pltpu.SMEM((1, 1, 2, slots), jnp.int32),
            pltpu.VMEM((sb, BLOCK), f32),
            pltpu.VMEM((sb, BLOCK), f32),
            pltpu.VMEM((tb, BLOCK), f32),
            pltpu.VMEM((tb, rows, BLOCK), jnp.bfloat16),
            pltpu.VMEM((tb, BLOCK, rows), jnp.bfloat16),
            pltpu.VMEM((width, tgt_len), f32),
            pltpu.VMEM((slots, BLOCK), f32),
            pltpu.VMEM((n_col, sb, BLOCK), f32),
            pltpu.VMEM((n_row, tb, BLOCK), f32),
            pltpu.VMEM((1, 128), jnp.int32),
            sem((n_col,)), sem((n_col,)), sem((n_col,)), sem((n_col,)),
            sem((n_row,)), sem((n_row,)), sem((n_col,)), sem((n_col,)),
            sem((n_col,)), sem((n_col,)), sem((n_col,)), sem((n_col,)),
            sem((2, n_col)), sem((2, n_col)), sem((6,)),
            *[pltpu.VMEM((BLOCK, BLOCK), f32)] * math.gcd(slots, 4),
        ],
        compiler_params=limit(
            collective_id=0, has_side_effects=True, vmem_limit_bytes=32 * 2**20
        ),
    )(
        in_hbm(src_latent),
        in_hbm(tgt_latent),
        in_hbm(g_start.reshape(1, tgt_len)),
        in_hbm(pairs.transpose(0, 1, 3, 2)),
        counts,
    )

    f_new, g_new, bary = pl.pallas_call(
        functools.partial(map_kernel, *sizes),
        out_shape=(
            jax.ShapeDtypeStruct((1, src_len), f32),
            jax.ShapeDtypeStruct((1, tgt_len), f32),
            jax.ShapeDtypeStruct((width, src_len), f32),
        ),
        in_specs=[smem, vmem, vmem, vmem, vmem, vmem],
        out_specs=(vmem, vmem, vmem),
        scratch_shapes=[
            pltpu.VMEM((sb, width + SUMS, BLOCK), f32),
            pltpu.VMEM((sb, 1, BLOCK), f32),
            pltpu.VMEM((BLOCK, BLOCK), jnp.bfloat16),
            pltpu.SMEM((3, n_col * slots), jnp.int32),
            *[pltpu.VMEM((BLOCK, BLOCK), f32)] * 2,
        ],
        compiler_params=limit(vmem_limit_bytes=40 * 2**20),
    )(all_meta, f_rows, g_rows, x_aug, all_g, all_y)
    return (f_new.reshape(src_len), g_new.reshape(tgt_len), bary)


def solution(mesh):
    in_specs = (
        P(None, "row"),
        P(None, "col"),
        P("col"),
        P("row", "col", None, None),
        P("row", "col"),
    )
    out_specs = (P("row"), P("col"), P(None, "row"))
    return jax.shard_map(
        functools.partial(body, mesh.shape["row"], mesh.shape["col"]),
        mesh=mesh, in_specs=in_specs, out_specs=out_specs, check_vma=False,
    )
```

```python
import functools
import math

import jax
import jax.numpy as jnp
from jax import lax
from jax.experimental import pallas as pl
from jax.experimental.pallas import tpu as pltpu
from jax.sharding import PartitionSpec as P

BLOCK = 512
HALF = 256
SUMS = 16
RUN = 64

epsilon = 0.01
very_low = -1e30
log2e = 1.0 / math.log(2.0)
MESH = pl.DeviceIdType.MESH


def dot(a, b, a_dim, b_dim):
    return lax.dot_general(
        a, b, (((a_dim,), (b_dim,)), ((), ())), preferred_element_type=jnp.float32
    )


def three(v):
    hi = v.astype(jnp.bfloat16).astype(jnp.float32)
    rest = v - hi
    mid = rest.astype(jnp.bfloat16).astype(jnp.float32)
    return hi, mid, rest - mid


def tail(rows, first, second):
    row = lax.broadcasted_iota(jnp.int32, (8, BLOCK), 0)
    out = jnp.zeros((8, BLOCK), jnp.float32)
    for start, value in ((0, first), (3, second)):
        if isinstance(value, tuple):
            for k in range(3):
                out = jnp.where(row == start + k, value[k], out)
        elif value:
            out = jnp.where((row >= start) & (row < start + 3), value, out)
    out = jnp.concatenate([out, jnp.zeros((rows - 8, BLOCK), jnp.float32)], axis=0)
    return out.astype(jnp.bfloat16)


def depth_of(width):
    return -(-(3 * width + 16) // 128) * 128


def scaled_rows(x, scale):
    return [part.astype(jnp.bfloat16) for part in three(x.astype(jnp.float32) * scale)]


def over_rows(op, x):
    while x.shape[0] > 8:
        ways = 4 if x.shape[0] % 32 == 0 else 2
        n = x.shape[0] // ways
        parts = [x[k * n : (k + 1) * n] for k in range(ways)]
        while len(parts) > 1:
            parts = [op(a, b) for a, b in zip(parts[::2], parts[1::2])]
        x = parts[0]
    return (jnp.max if op is jnp.maximum else jnp.sum)(x, axis=0, keepdims=True)


def put_scores(buf, lhs, rhs_ref, block):
    for h in range(BLOCK // HALF):
        at = slice(h * HALF, (h + 1) * HALF)
        buf[:, at] = dot(lhs, rhs_ref[block, :, at], 1, 0)


def column_top(buf, at):
    top = buf[0:RUN, at]
    for k in range(RUN, BLOCK, RUN):
        top = jnp.maximum(top, buf[k : k + RUN, at])
    return over_rows(jnp.maximum, top)


def column_lse(buf):
    out = []
    for h in range(BLOCK // HALF):
        at = slice(h * HALF, (h + 1) * HALF)
        top = column_top(buf, at)
        total = jnp.zeros((RUN, HALF), jnp.float32)
        for k in range(0, BLOCK, RUN):
            total = total + jnp.exp2(buf[k : k + RUN, at] - top)
        out.append(top + jnp.log(over_rows(jnp.add, total)) * log2e)
    return jnp.concatenate(out, axis=1)


def merge_slots(lse, ids, block):
    own = ids == block
    top = jnp.max(jnp.where(own, lse, very_low), axis=0, keepdims=True)
    total = jnp.sum(jnp.where(own, jnp.exp2(lse - top), 0.0), axis=0, keepdims=True)
    return jnp.where(total > 0.0, top + jnp.log(jnp.maximum(total, 1e-30)) * log2e, very_low)


def repeat(n, step, state=None):
    if n > 8:
        return lax.fori_loop(0, n, step, state)
    for k in range(n):
        state = step(k, state)
    return state


def merge_devices(ref, n):
    top = repeat(n, lambda c, t: jnp.maximum(t, ref[c]), ref[0])
    total = repeat(n, lambda c, t: t + jnp.exp2(ref[c] - top), jnp.zeros(top.shape, jnp.float32))
    return top + jnp.log(total) * log2e


def potentials_kernel(
    n_row, n_col, sb, tb, slots, width,
    x_hbm, y_hbm, g_hbm, pairs_hbm, counts_ref,
    f_rows, g_rows, x_aug, all_g_ref, all_y_ref, all_meta_ref,
    x_ref, y_ref, g_ref, pairs_ref, lse_f_ref, merged_f, sq_x, sq_y, y_aug, y_flip, y_wide, slot_lse, from_col, from_row, meta,
    meta_send, meta_recv, f_send, f_recv, g_send, g_recv, h_send, h_recv,
    y_send, y_recv, x_send, x_recv, z_send, z_recv, local_sem, *bufs,
):
    row = lax.axis_index("row")
    col = lax.axis_index("col")
    low = lax.rem(row, 2)
    high = lax.rem(row, 4) // 2
    across = row + 2 - 4 * high
    sibling = row + 1 - 2 * low
    quarter = width // 4

    def rows_of(high, low):
        return pl.ds(pl.multiple_of((2 * high + low) * quarter, quarter), quarter)

    deep = 3 * width
    extra = depth_of(width) - deep

    get_y = pltpu.make_async_copy(y_hbm, y_ref, local_sem.at[2])
    get_y.start()
    get_x = pltpu.make_async_copy(x_hbm, x_ref, local_sem.at[3])
    get_x.start()

    get_g = pltpu.make_async_copy(g_hbm, g_ref, local_sem.at[4])
    get_g.start()
    get_pairs = pltpu.make_async_copy(pairs_hbm, pairs_ref, local_sem.at[5])
    get_pairs.start()

    barrier = pltpu.get_barrier_semaphore()

    def over(n, me, do):
        def step(d, carry):
            do(lax.rem(me + d, n))
            return carry

        lax.fori_loop(1, n, step, 0)

    over(n_col, col, lambda c: pl.semaphore_signal(
        barrier, inc=1, device_id=(row, c), device_id_type=MESH))
    over(n_row, row, lambda r: pl.semaphore_signal(
        barrier, inc=1, device_id=(r, col), device_id_type=MESH))

    def to_col(src, dst, send, recv, c):
        return pltpu.make_async_remote_copy(
            src_ref=src, dst_ref=dst.at[col], send_sem=send.at[c], recv_sem=recv.at[col],
            device_id=(row, c), device_id_type=MESH)

    def from_col_of(dst, send, recv, c):
        return pltpu.make_async_remote_copy(
            src_ref=dst.at[c], dst_ref=dst.at[c], send_sem=send.at[c], recv_sem=recv.at[c],
            device_id=(row, c), device_id_type=MESH)

    get_pairs.wait()
    count = counts_ref[0, 0]
    lane = lax.broadcasted_iota(jnp.int32, (1, 128), 1)
    slot = lax.broadcasted_iota(jnp.int32, (slots, BLOCK), 0)
    ids_s = jnp.full((slots, BLOCK), -1, jnp.int32)
    ids_t = jnp.full((slots, BLOCK), -1, jnp.int32)
    packed = jnp.where(lane == 2 * slots, count, 0)
    for p in range(slots):
        ids_s = jnp.where(slot == p, pairs_ref[0, 0, 0, p], ids_s)
        ids_t = jnp.where(slot == p, pairs_ref[0, 0, 1, p], ids_t)
        packed = jnp.where(lane == 2 * p, pairs_ref[0, 0, 0, p], packed)
        packed = jnp.where(lane == 2 * p + 1, pairs_ref[0, 0, 1, p], packed)
    ids_s = jnp.where(slot < count, ids_s, -1)
    ids_t = jnp.where(slot < count, ids_t, -1)
    meta[...] = packed

    def prepare_x(s, carry):
        x = x_ref[:, s * BLOCK : (s + 1) * BLOCK]
        for k, part in enumerate(scaled_rows(x, 2.0 * log2e / (width * epsilon))):
            x_aug[s, k * width : (k + 1) * width, :] = part
        x_aug[s, deep:, :] = tail(extra, 0.0, 1.0)
        xf = x.astype(jnp.float32)
        sq_x[s : s + 1, :] = jnp.sum(xf * xf, axis=0, keepdims=True) * (1.0 / width)
        return carry

    def prepare_y(t, carry):
        at = slice(t * BLOCK, (t + 1) * BLOCK)
        y = y_ref[:, at]
        yf = y.astype(jnp.float32)
        y_wide[:, at] = yf
        for k in range(3):
            y_aug[t, k * width : (k + 1) * width, :] = y
        sq = jnp.sum(yf * yf, axis=0, keepdims=True) * (1.0 / width)
        sq_y[t : t + 1, :] = sq
        v = (g_ref[:, at] - sq) * (log2e / epsilon)
        y_aug[t, deep:, :] = tail(extra, 1.0, three(v))
        y_flip[t] = y_aug[t].T
        return carry

    get_y.wait()
    get_g.wait()
    for t in range(tb):
        prepare_y(t, 0)
    get_x.wait()
    for s in range(sb):
        prepare_x(s, 0)

    def y_copy(source, c):
        return pltpu.make_async_remote_copy(
            src_ref=y_wide.at[rows_of(high, low)],
            dst_ref=all_y_ref.at[source, rows_of(high, low)],
            send_sem=y_send.at[c], recv_sem=y_recv.at[source],
            device_id=(row, c), device_id_type=MESH)

    pl.semaphore_wait(barrier, n_col + n_row - 2)
    over(n_col, col, lambda c: y_copy(col, c).start())
    over(n_col, col, lambda c: to_col(meta, all_meta_ref, meta_send, meta_recv, c).start())

    local_y = pltpu.make_async_copy(y_wide, all_y_ref.at[col], local_sem.at[0])
    local_y.start()
    local_meta = pltpu.make_async_copy(meta, all_meta_ref.at[col], local_sem.at[1])
    local_meta.start()

    group = math.gcd(slots, 8)

    def in_turn(put, q):
        put(0)
        for k in range(group):
            if k + 1 < group:
                put(k + 1)
            slot_lse[pl.ds(q * group + k, 1), :] = column_lse(bufs[k])

    def source_step(q, carry):
        def put(k):
            p = q * group + k
            put_scores(bufs[k], y_flip[pairs_ref[0, 0, 1, p]], x_aug, pairs_ref[0, 0, 0, p])

        in_turn(put, q)
        return carry

    lax.fori_loop(0, slots // group, source_step, 0)
    lse = slot_lse[...]
    for s in range(sb):
        lse_f_ref[s : s + 1, :] = merge_slots(lse, ids_s, s)
    from_col[col] = lse_f_ref[...]

    over(n_col, col, lambda c: to_col(lse_f_ref, from_col, f_send, f_recv, c).start())

    def x_copy(source, high):
        return pltpu.make_async_remote_copy(
            src_ref=all_y_ref.at[source, rows_of(high, low)],
            dst_ref=all_y_ref.at[source, rows_of(high, low)],
            send_sem=x_send.at[source], recv_sem=x_recv.at[source],
            device_id=(across, col), device_id_type=MESH)

    def pass_across(c):
        y_copy(c, c).wait_recv()
        x_copy(c, high).start()

    over(n_col, col, pass_across)
    over(n_col, col, lambda c: from_col_of(from_col, f_send, f_recv, c).wait_recv())

    merged = merge_devices(from_col, n_col)
    merged_f[...] = merged
    for s in range(sb):
        u = -math.log2(sb * BLOCK * n_row) - merged[s : s + 1, :]
        x_aug[s, deep:, :] = tail(extra, three(u), 0.0)

    def target_step(q, carry):
        def put(k):
            p = q * group + k
            put_scores(bufs[k], x_aug[pairs_ref[0, 0, 0, p]].T, y_aug, pairs_ref[0, 0, 1, p])

        in_turn(put, q)
        return carry

    lax.fori_loop(0, slots // group, target_step, 0)
    lse = slot_lse[...]
    for t in range(tb):
        from_row[row, t : t + 1, :] = merge_slots(lse, ids_t, t)

    def g_copy(source, r):
        return pltpu.make_async_remote_copy(
            src_ref=from_row.at[source], dst_ref=from_row.at[source],
            send_sem=g_send.at[r], recv_sem=g_recv.at[source],
            device_id=(r, col), device_id_type=MESH)

    over(n_row, row, lambda r: g_copy(row, r).start())

    def z_copy(source, k, high, low):
        return pltpu.make_async_remote_copy(
            src_ref=all_y_ref.at[source, rows_of(high, low)],
            dst_ref=all_y_ref.at[source, rows_of(high, low)],
            send_sem=z_send.at[k, source], recv_sem=z_recv.at[k, source],
            device_id=(sibling, col), device_id_type=MESH)

    def pass_to_sibling(c):
        x_copy(c, 1 - high).wait_recv()
        z_copy(c, 0, high, low).start()
        z_copy(c, 1, 1 - high, low).start()

    def wait_from_sibling(c):
        z_copy(c, 0, high, 1 - low).wait_recv()
        z_copy(c, 1, 1 - high, 1 - low).wait_recv()

    def wait_to_sibling(c):
        z_copy(c, 0, high, low).wait_send()
        z_copy(c, 1, 1 - high, low).wait_send()

    over(n_col, col, pass_to_sibling)
    over(n_row, row, lambda r: g_copy(r, r).wait_recv())
    all_g_ref[col] = merge_devices(from_row, n_row)

    def h_copy(source, c):
        return pltpu.make_async_remote_copy(
            src_ref=all_g_ref.at[source], dst_ref=all_g_ref.at[source],
            send_sem=h_send.at[c], recv_sem=h_recv.at[source],
            device_id=(row, c), device_id_type=MESH)

    over(n_col, col, lambda c: h_copy(col, c).start())

    log_ns = math.log(sb * BLOCK * n_row)
    log_nt = math.log(tb * BLOCK * n_col)
    f_rows[...] = sq_x[...] - epsilon * (log_ns + merged_f[...] / log2e)
    g_rows[...] = sq_y[...] - epsilon * (log_nt + all_g_ref[col] / log2e)
    for s in range(sb):
        x_aug[s, deep:, :] = tail(extra, 0.0, 1.0)


    over(n_col, col, lambda c: to_col(lse_f_ref, from_col, f_send, f_recv, c).wait_send())
    over(n_col, col, lambda c: y_copy(col, c).wait_send())
    over(n_col, col, lambda c: to_col(meta, all_meta_ref, meta_send, meta_recv, c).wait_send())
    over(n_col, col, lambda c: from_col_of(all_meta_ref, meta_send, meta_recv, c).wait_recv())
    over(n_col, col, lambda c: x_copy(c, high).wait_send())
    over(n_row, row, lambda r: g_copy(row, r).wait_send())
    local_y.wait()
    local_meta.wait()
    over(n_col, col, wait_from_sibling)
    over(n_col, col, wait_to_sibling)
    over(n_col, col, lambda c: h_copy(col, c).wait_send())
    over(n_col, col, lambda c: h_copy(c, c).wait_recv())


def map_kernel(
    n_row, n_col, sb, tb, slots, width,
    meta_ref, f_rows, g_rows, x_aug, all_g_ref, all_y_ref,
    f_ref, g_ref, bary_ref,
    acc, peak, weights, work, *bufs,
):
    extra = depth_of(width) - 3 * width
    for rows, out, n in ((f_rows, f_ref, sb), (g_rows, g_ref, tb)):
        for k in range(n):
            out[:, k * BLOCK : (k + 1) * BLOCK] = rows[k : k + 1, :]
    acc[...] = jnp.zeros_like(acc)
    peak[...] = jnp.full(peak.shape, very_low, jnp.float32)

    def list_column(c, at):
        def put(p, at):
            work[0, at] = c
            work[1, at] = meta_ref[c, 0, 2 * p]
            work[2, at] = meta_ref[c, 0, 2 * p + 1]
            return at + 1

        return lax.fori_loop(0, meta_ref[c, 0, 2 * slots], put, at)

    tiles = lax.fori_loop(0, n_col, list_column, 0)

    def place(n):
        at = jnp.minimum(n, tiles - 1)
        return work[0, at], work[1, at], work[2, at]

    def targets(c, t):
        off = pl.multiple_of(t * BLOCK, BLOCK)
        return all_y_ref[c, :, pl.ds(off, BLOCK)].astype(jnp.bfloat16)

    def put(n, buf):
        c, s, t = place(n)
        y = targets(c, t)
        w = -all_g_ref[c, pl.ds(t, 1), :]
        lhs = jnp.concatenate([y, y, y, tail(extra, 0.0, three(w))], axis=0).T
        put_scores(buf, lhs, x_aug, s)

    def use(n, buf):
        c, s, t = place(n)
        sums = jnp.concatenate([targets(c, t), jnp.ones((SUMS, BLOCK), jnp.bfloat16)], axis=0)
        for h in range(BLOCK // HALF):
            at = slice(h * HALF, (h + 1) * HALF)
            top = column_top(buf, at)
            for k in range(0, BLOCK, RUN):
                run = slice(k, k + RUN)
                weights[run, at] = jnp.exp2(buf[run, at] - top).astype(jnp.bfloat16)
            part = dot(sums, weights[:, at], 1, 0)
            top = jnp.where(n < tiles, top, very_low)
            old = peak[s, :, at]
            new = jnp.maximum(old, top)
            acc[s, :, at] = acc[s, :, at] * jnp.exp2(old - new) + part * jnp.exp2(top - new)
            peak[s, :, at] = new

    put(0, bufs[0])

    def run(first, steps, pairs):
        def step(q, carry):
            for k in range(pairs):
                n = first + 2 * (q * pairs + k)
                put(n + 1, bufs[1])
                use(n, bufs[0])
                put(n + 2, bufs[0])
                use(n + 1, bufs[1])
            return carry

        lax.fori_loop(0, steps, step, 0)

    fours = tiles // 4
    run(0, fours, 2)
    run(4 * fours, (tiles - 4 * fours + 1) // 2, 1)

    for s in range(sb):
        bary_ref[:, s * BLOCK : (s + 1) * BLOCK] = acc[s, :width, :] * (
            1.0 / acc[s, width : width + 1, :])


def in_hbm(x):
    return pltpu.with_memory_space_constraint(x, pltpu.HBM)


def body(n_row, n_col, src_latent, tgt_latent, g_start, pairs, counts):
    width, src_len = src_latent.shape
    tgt_len = tgt_latent.shape[1]
    slots = pairs.shape[2]
    sb, tb = src_len // BLOCK, tgt_len // BLOCK
    rows = depth_of(width)
    sizes = (n_row, n_col, sb, tb, slots, width)
    vmem = pl.BlockSpec(memory_space=pltpu.VMEM)
    smem = pl.BlockSpec(memory_space=pltpu.SMEM)
    hbm = pl.BlockSpec(memory_space=pltpu.HBM)
    anywhere = pl.BlockSpec(memory_space=pl.ANY)
    limit = pltpu.CompilerParams
    f32 = jnp.float32
    sem = pltpu.SemaphoreType.DMA

    f_rows, g_rows, x_aug, all_g, all_y, all_meta = pl.pallas_call(
        functools.partial(potentials_kernel, *sizes),
        out_shape=(
            jax.ShapeDtypeStruct((sb, BLOCK), f32),
            jax.ShapeDtypeStruct((tb, BLOCK), f32),
            jax.ShapeDtypeStruct((sb, rows, BLOCK), jnp.bfloat16),
            jax.ShapeDtypeStruct((n_col, tb, BLOCK), f32),
            jax.ShapeDtypeStruct((n_col, width, tgt_len), f32),
            jax.ShapeDtypeStruct((n_col, 1, 128), jnp.int32),
        ),
        in_specs=[hbm, hbm, hbm, hbm, smem],
        out_specs=(vmem, vmem, vmem, vmem, anywhere, vmem),
        scratch_shapes=[
            pltpu.VMEM((width, src_len), jnp.bfloat16),
            pltpu.VMEM((width, tgt_len), jnp.bfloat16),
            pltpu.VMEM((1, tgt_len), f32),
            pltpu.SMEM((1, 1, 2, slots), jnp.int32),
            pltpu.VMEM((sb, BLOCK), f32),
            pltpu.VMEM((sb, BLOCK), f32),
            pltpu.VMEM((sb, BLOCK), f32),
            pltpu.VMEM((tb, BLOCK), f32),
            pltpu.VMEM((tb, rows, BLOCK), jnp.bfloat16),
            pltpu.VMEM((tb, BLOCK, rows), jnp.bfloat16),
            pltpu.VMEM((width, tgt_len), f32),
            pltpu.VMEM((slots, BLOCK), f32),
            pltpu.VMEM((n_col, sb, BLOCK), f32),
            pltpu.VMEM((n_row, tb, BLOCK), f32),
            pltpu.VMEM((1, 128), jnp.int32),
            sem((n_col,)), sem((n_col,)), sem((n_col,)), sem((n_col,)),
            sem((n_row,)), sem((n_row,)), sem((n_col,)), sem((n_col,)),
            sem((n_col,)), sem((n_col,)), sem((n_col,)), sem((n_col,)),
            sem((2, n_col)), sem((2, n_col)), sem((6,)),
            *[pltpu.VMEM((BLOCK, BLOCK), f32)] * math.gcd(slots, 8),
        ],
        compiler_params=limit(
            collective_id=0, has_side_effects=True, vmem_limit_bytes=32 * 2**20
        ),
    )(
        in_hbm(src_latent),
        in_hbm(tgt_latent),
        in_hbm(g_start.reshape(1, tgt_len)),
        in_hbm(pairs.transpose(0, 1, 3, 2)),
        counts,
    )

    f_new, g_new, bary = pl.pallas_call(
        functools.partial(map_kernel, *sizes),
        out_shape=(
            jax.ShapeDtypeStruct((1, src_len), f32),
            jax.ShapeDtypeStruct((1, tgt_len), f32),
            jax.ShapeDtypeStruct((width, src_len), f32),
        ),
        in_specs=[smem, vmem, vmem, vmem, vmem, vmem],
        out_specs=(vmem, vmem, vmem),
        scratch_shapes=[
            pltpu.VMEM((sb, width + SUMS, BLOCK), f32),
            pltpu.VMEM((sb, 1, BLOCK), f32),
            pltpu.VMEM((BLOCK, BLOCK), jnp.bfloat16),
            pltpu.SMEM((3, n_col * slots), jnp.int32),
            *[pltpu.VMEM((BLOCK, BLOCK), f32)] * 2,
        ],
        compiler_params=limit(vmem_limit_bytes=40 * 2**20),
    )(all_meta, f_rows, g_rows, x_aug, all_g, all_y)
    return (f_new.reshape(src_len), g_new.reshape(tgt_len), bary)


def solution(mesh):
    in_specs = (
        P(None, "row"),
        P(None, "col"),
        P("col"),
        P("row", "col", None, None),
        P("row", "col"),
    )
    out_specs = (P("row"), P("col"), P(None, "row"))
    return jax.shard_map(
        functools.partial(body, mesh.shape["row"], mesh.shape["col"]),
        mesh=mesh, in_specs=in_specs, out_specs=out_specs, check_vma=False,
    )
```
